32 devices in a mesh: lat: 8 (over y, x, core), lon: 4 (over z).
Axes of the slice: x: 2, y: 2, z: 4, core: 2. Of those that a mesh axis runs over, the one named last changes fastest.
Arguments:
- signal: float32 [16, 1440, 384], P('lat', 'lon'), may hold values from -6 to 6
- band_rows: int32 [8], replicated, may hold values from 1 to 2, 12 in all
- filter_modes: float32 [16, 3, 3, 2, 720], P('lat'), may hold values from -3 to 3
- mixing: float32 [3, 384, 384], replicated, may hold values from -0.1875 to 0.1875
- cotangent: float32 [16, 1440, 384], P('lat', 'lon'), may hold values from -6 to 6
Outputs:
- output: float32 [16, 1440, 384], P('lat', 'lon')
- grad_signal: float32 [16, 1440, 384], P('lat', 'lon')
- weight_grad: float32 [3, 384, 384], replicated
The draws below stay inside these ranges and needn't reach their ends.
Inputs may be any that keep to these rules, and one draw needn't show every extreme that they name: Band b uses row slots 0 to band_rows[b] - 1 of its 2 slots; the other slots hold values that no output reads. Some band is full.
All inputs are finite; a program needn't handle non-finite values.
Results may differ from the reference program's by a relative error of at most 0.0001.
Values sent between devices are 32-bit elements; how exact they have to be, the bound alone decides.
No kernel may reach another device: no remote copies, remote signals or barrier semaphores. Data moves between devices by JAX's collectives and lax.ppermute only.
A program may use at most 128 MiB of HBM per device.

```python
import math
import jax
import jax.numpy as jnp
import numpy as np
from jax import lax

LON = 1440
C = 384
K = 3
RB = 2
MODES = 720
NROWS = 16
N_LAT = 8


def block_scale(own_key, shape, shards, least, top_value):
    level = 1.0
    for position, blocks in shards:
        draws = jax.random.uniform(jax.random.fold_in(jax.random.fold_in(own_key, 6), position), (blocks,), jnp.float32, least / len(shards), top_value / len(shards))
        level = level * jnp.repeat(jnp.exp(draws), shape[position] // blocks).reshape((-1,) + (1,) * (len(shape) - 1 - position))
    return level


def profile(count, total, reach, slope):
    weights = [(1 << 20) // math.isqrt(rank ** slope) + 1 for rank in range(2, count + 1)]
    rest, given = total - reach - (count - 1), [1] * (count - 1)
    while rest > 0:
        free = [i for i in range(count - 1) if given[i] < reach]
        mass, remaining = sum([weights[i] for i in free]), rest
        for i in free:
            extra = min(reach - given[i], max(1, remaining * weights[i] // mass), rest)
            given[i] = given[i] + extra
            rest = rest - extra
    return np.array([reach] + given)


def ragged(own_key, count, total, reach, skew):
    if count == 2:
        one = jax.random.randint(own_key, (), max(1, total - reach), min(reach, total - 1) + 1)
        return jnp.stack([one, total - one])
    tallies = jnp.asarray(profile(count, total, reach, skew), jnp.int32)
    couples = (count - 1) // 2
    giver, taker = tallies[1:1 + 2 * couples:2], tallies[2:2 + 2 * couples:2]
    slack = jnp.minimum(giver - 1, reach - taker)
    passed = jax.random.randint(jax.random.fold_in(own_key, 1), (couples,), 0, 1 << 20) % (slack + 1)
    tallies = tallies.at[1:1 + 2 * couples:2].set(giver - passed).at[2:2 + 2 * couples:2].set(taker + passed)
    return tallies[jax.random.permutation(jax.random.fold_in(own_key, 2), count)]


def centred(own_key, dims, scale, reach, split=(), held_as=jnp.bfloat16):
    factor_of = block_scale(own_key, dims, split, -0.22, 0.18) if split else 1.0
    values = jax.random.normal(own_key, dims, jnp.float32) * scale * factor_of
    return jnp.minimum(jnp.maximum(values, -reach), reach).astype(held_as)


def setup_inputs(seed: int = 0) -> dict:
    keys = jax.random.split(jax.random.key(seed), 6)
    return {
        "signal": centred(keys[0], (NROWS, LON, C), 1.0, 6.0, ((0, 8), (1, 4)), jnp.float32),
        "band_rows": ragged(keys[1], N_LAT, N_LAT * RB * 3 // 4, RB, 2).astype(jnp.int32),
        "filter_modes": centred(keys[2], (NROWS, 3, K, 2, MODES), 0.5, 3.0, ((0, 8),), jnp.float32),
        "mixing": centred(keys[3], (K, C, C), (K * C) ** -0.5, 0.1875, (), jnp.float32),
        "cotangent": centred(keys[4], (NROWS, LON, C), 1.0, 6.0, ((0, 8), (1, 4)), jnp.float32),
    }


def reference(signal, band_rows, filter_modes, mixing, cotangent):
    slot_total = N_LAT * RB
    slot_index = jnp.arange(slot_total, dtype=jnp.int32)
    band_index = slot_index // RB
    row_index = slot_index % RB
    counts = band_rows[band_index]
    earlier = jnp.concatenate([jnp.ones((1,), jnp.int32), band_rows[:-1]])[band_index]
    prev_index = jnp.where(row_index > 0, slot_index - 1, (band_index - 1) * RB + earlier - 1)
    prev_valid = (row_index > 0) | (band_index > 0)
    next_index = jnp.where(row_index + 1 < counts, slot_index + 1, (band_index + 1) * RB)
    next_valid = (row_index + 1 < counts) | (band_index < N_LAT - 1)
    prev_index = jnp.clip(prev_index, 0, slot_total - 1).astype(jnp.int32)
    next_index = jnp.clip(next_index, 0, slot_total - 1).astype(jnp.int32)
    live_mask = row_index < counts
    coefficient = filter_modes[:, :, :, 0, :] + 1j * filter_modes[:, :, :, 1, :]

    def conv_layer(field_in, weights):
        spectrum = jnp.fft.rfft(field_in, axis=1)[:, :MODES, :]
        lower_rows = jnp.where(prev_valid[:, None, None], spectrum[prev_index], 0.0)
        upper_rows = jnp.where(next_valid[:, None, None], spectrum[next_index], 0.0)
        stacked = jnp.stack([lower_rows, spectrum, upper_rows], axis=1)
        result = jnp.zeros(field_in.shape, field_in.dtype)
        for basis in range(K):
            mixed_modes = jnp.einsum('rdm,rdmc->rmc', coefficient[:, :, basis, :], stacked)
            padded = jnp.concatenate([mixed_modes, jnp.zeros((slot_total, 1, C), mixed_modes.dtype)], axis=1)
            cycle_block = jnp.fft.irfft(padded, n=LON, axis=1)
            result = result + jnp.einsum('rnc,co->rno', cycle_block, weights[basis], precision=lax.Precision.HIGHEST)
        return jnp.where(live_mask[:, None, None], result, 0.0)
    output, pullback = jax.vjp(conv_layer, signal, mixing)
    grad_signal, weight_grad = pullback(cotangent)
    return (output, grad_signal, weight_grad)
```

```python
import math

import jax
import jax.numpy as jnp
import numpy as np
from jax import lax
from jax.sharding import PartitionSpec as P

AXES = ("lat", "lon")
SLOTS = 4
HIGH = lax.Precision.HIGH


class Layout:
    def __init__(self, lat, lon):
        self.lat, self.lon, self.pairs = lat, lon, lat // 2
        self.chips = lon // SLOTS
        self.share = 2 * self.chips

    def device(self, band, z):
        return band * self.lon + z

    def place(self, pair, rho, h):
        v = rho * self.chips + h // 2
        z = v if pair % 2 == 0 else self.lon - 1 - v
        return self.device(2 * pair + h % 2, z)

    def inward(self, t):
        pairs = []
        for band in range(self.lat):
            for z in range(self.lon):
                r = (z // self.share) ^ t
                dst = self.place(band // 2, 2 * (band % 2) + r, z % self.share)
                pairs.append((self.device(band, z), dst))
        return pairs

    def slots(self):
        for pair in range(self.pairs):
            for rho in range(SLOTS):
                for h in range(self.share):
                    yield pair, rho, h

    def within(self, g):
        return [(self.place(p, rho, h), self.place(p, rho, h ^ g)) for p, rho, h in self.slots()]

    def upward(self):
        pairs = []
        for p, rho, h in self.slots():
            q, sigma = (p, rho + 1) if rho + 1 < SLOTS else (p + 1, 0)
            if q < self.pairs:
                pairs.append((self.place(p, rho, h), self.place(q, sigma, h)))
        return pairs


def flipped(pairs):
    return [(b, a) for a, b in pairs]


def tables(length, modes, lon, share):
    n = np.arange(length)
    m = np.arange(modes)
    angle = (n[:, None] * m[None, :] % length) * (2.0 * math.pi / length)
    root = np.sqrt(np.where(m == 0, 1.0, 2.0) / length)
    cosine = (np.cos(angle) * root).reshape(lon, length // lon, modes)
    sine = (-np.sin(angle) * root).reshape(lon, length // lon, modes)
    width = modes // share
    out = []
    for h in range(share):
        order = [b * share + (h ^ g) for g in range(share) for b in range(2)]
        part = slice(h * width, (h + 1) * width)
        out.append(np.concatenate([cosine[order][:, :, part], sine[order][:, :, part]], axis=2).reshape(length, 2 * width))
    return np.stack(out).astype(np.float32)


def make_local(lat, lon):
    lay = Layout(lat, lon)
    share = lay.share

    def send(x, pairs):
        return lax.ppermute(x, AXES, pairs)

    def local(signal, band_rows, filter_modes, mixing, cotangent):
        channels = signal.shape[2]
        part_len = signal.shape[1]
        length = part_len * lon
        modes = filter_modes.shape[-1]
        basis = mixing.shape[0]
        width = modes // share

        band = lax.axis_index("lat")
        z = lax.axis_index("lon")
        core = band % 2
        v = jnp.where((band // 2) % 2 == 0, z, lon - 1 - z)
        rho = v // lay.chips
        h = (v % lay.chips) * 2 + core
        r_held = rho % 2
        live = lax.dynamic_index_in_dim(band_rows, band, 0, keepdims=False)
        full = live == 2
        high_z = z // share

        table = lax.dynamic_index_in_dim(jnp.asarray(tables(length, modes, lon, share)), h, 0, keepdims=False)

        def enter(x):
            got = []
            for t in range(2):
                row = jnp.minimum(high_z ^ t, live - 1)
                got.append(send(lax.dynamic_index_in_dim(x, row, 0, keepdims=False), lay.inward(t)))
            own = jnp.stack([jnp.where(r_held == 0, got[0], got[1]), jnp.where(r_held == 0, got[1], got[0])])
            rows = [own] + [send(own, lay.within(g)) for g in range(1, share)]
            rows = jnp.concatenate(rows, axis=0).reshape(length, channels)
            return jnp.einsum("nf,nc->fc", table, rows, precision=HIGH)

        def leave(spec):
            y = jnp.einsum("nf,fc->nc", table, spec, precision=HIGH).reshape(share, 2, part_len, channels)
            own = y[0]
            for g in range(1, share):
                own = own + send(y[g], lay.within(g))
            got = []
            for t in range(2):
                block = jnp.where((r_held ^ t) == 0, own[0], own[1])
                got.append(send(block, flipped(lay.inward(t))))
            first = jnp.where(high_z == 0, got[0], got[1])
            second = jnp.where(high_z == 0, got[1], got[0])
            return jnp.stack([jnp.where(full, first, first + second), jnp.where(full, second, 0.0)])

        f = filter_modes
        ladder = [(i, i + 1) for i in range(lat - 1)]
        below = lax.ppermute(jnp.where(full, f[1, 2], f[0, 2]), "lat", ladder)
        above = lax.ppermute(f[0, 0], "lat", flipped(ladder))
        nil = jnp.zeros_like(below)
        is_first = r_held == 0
        ahead = [
            jnp.where(is_first, f[0, 0], jnp.where(full, f[1, 0], nil)),
            jnp.where(is_first, f[0, 1], jnp.where(full, f[1, 1], nil)),
            jnp.where(is_first, jnp.where(full, f[0, 2], nil), jnp.where(full, f[1, 2], f[0, 2])),
        ]
        back = [
            jnp.where(is_first, below, jnp.where(full, f[0, 2], nil)),
            jnp.where(is_first, f[0, 1], jnp.where(full, f[1, 1], nil)),
            jnp.where(is_first, jnp.where(full, f[1, 0], nil), above),
        ]
        conj = jnp.array([1.0, -1.0], jnp.float32)[None, None, :, None]
        both = jnp.stack([jnp.stack(ahead), jnp.stack(back) * conj])
        both = both.reshape(2 * 3 * basis * 2, modes)
        swap = [(i, i ^ 1) for i in range(lat)]
        theirs = lax.ppermute(lax.dynamic_slice_in_dim(both, (h ^ 1) * width, width, 1), "lat", swap)
        mine = lax.dynamic_slice_in_dim(both, h * width, width, 1)
        coef = jnp.where(rho // 2 == core, mine, theirs).reshape(2, 3, basis, 2, width)

        def mix(spec, coef, weights):
            lower = send(spec, lay.upward())
            upper = send(spec, flipped(lay.upward()))
            real, imag = [], []
            for k in range(basis):
                re, im = 0.0, 0.0
                for d, row in enumerate((lower, spec, upper)):
                    pr, pi = coef[d, k, 0][:, None], coef[d, k, 1][:, None]
                    xr, xi = row[:width], row[width:]
                    re = re + (pr * xr - pi * xi)
                    im = im + (pr * xi + pi * xr)
                real.append(re)
                imag.append(im)
            filtered = jnp.concatenate([jnp.concatenate(real, axis=1), jnp.concatenate(imag, axis=1)], axis=0)
            return filtered, jnp.einsum("fc,co->fo", filtered, weights, precision=HIGH)

        s_spec = enter(signal)
        g_spec = enter(cotangent)
        filtered, o_spec = mix(s_spec, coef[0], mixing.reshape(basis * channels, channels))
        output = leave(o_spec)
        _, b_spec = mix(g_spec, coef[1], jnp.transpose(mixing, (0, 2, 1)).reshape(basis * channels, channels))
        grad_signal = leave(b_spec)
        term = jnp.einsum("fc,fo->co", filtered, g_spec, precision=HIGH)

        bits = int(math.log2(lat))
        for i in range(bits):
            bit = (band >> i) & 1
            half = term.shape[0] // 2
            term = term.reshape(2, half, channels)
            keep = lax.dynamic_index_in_dim(term, bit, 0, keepdims=False)
            give = lax.dynamic_index_in_dim(term, 1 - bit, 0, keepdims=False)
            term = keep + lax.ppermute(give, "lat", [(a, a ^ (1 << i)) for a in range(lat)])
        shape = term.shape
        parts = term.reshape(lon, -1, 128) if term.size % (lon * 128) == 0 else term.reshape(lon, 1, -1)
        total = lax.dynamic_index_in_dim(parts, z, 0, keepdims=False)
        for g in range(1, lon):
            piece = lax.dynamic_index_in_dim(parts, z ^ g, 0, keepdims=False)
            total = total + lax.ppermute(piece, "lon", [(a, a ^ g) for a in range(lon)])
        gathered = jnp.zeros_like(parts)
        gathered = lax.dynamic_update_index_in_dim(gathered, total, z, 0)
        for g in range(1, lon):
            piece = lax.ppermute(total, "lon", [(a, a ^ g) for a in range(lon)])
            gathered = lax.dynamic_update_index_in_dim(gathered, piece, z ^ g, 0)
        term = gathered.reshape(shape)
        for i in reversed(range(bits)):
            bit = (band >> i) & 1
            other = lax.ppermute(term, "lat", [(a, a ^ (1 << i)) for a in range(lat)])
            term = jnp.concatenate([jnp.where(bit == 0, term, other), jnp.where(bit == 0, other, term)], axis=0)
        weight_grad = term.reshape(mixing.shape)
        return output, grad_signal, weight_grad

    return local


def solution(mesh):
    lat, lon = mesh.shape["lat"], mesh.shape["lon"]
    grid = P("lat", "lon", None)
    return jax.shard_map(
        make_local(lat, lon),
        mesh=mesh,
        in_specs=(grid, P(), P("lat", None, None, None, None), P(), grid),
        out_specs=(grid, grid, P()),
        check_vma=False,
    )
```

```python
import math

import jax
import jax.numpy as jnp
import numpy as np
from jax import lax
from jax.experimental import pallas as pl
from jax.experimental.pallas import tpu as pltpu
from jax.sharding import PartitionSpec as P

AXES = ("lat", "lon")
SLOTS = 4
VMEM = 48 * 2**20
BF16 = jnp.bfloat16


class Layout:
    def __init__(self, lat, lon):
        self.lat, self.lon, self.pairs = lat, lon, lat // 2
        self.chips = lon // SLOTS
        self.share = 2 * self.chips

    def device(self, band, z):
        return band * self.lon + z

    def place(self, pair, rho, h):
        v = rho * self.chips + h // 2
        z = v if pair % 2 == 0 else self.lon - 1 - v
        return self.device(2 * pair + h % 2, z)

    def inward(self, t):
        pairs = []
        for band in range(self.lat):
            for z in range(self.lon):
                r = (z // self.share) ^ t
                dst = self.place(band // 2, 2 * (band % 2) + r, z % self.share)
                pairs.append((self.device(band, z), dst))
        return pairs

    def slots(self):
        for pair in range(self.pairs):
            for rho in range(SLOTS):
                for h in range(self.share):
                    yield pair, rho, h

    def within(self, g):
        return [(self.place(p, rho, h), self.place(p, rho, h ^ g)) for p, rho, h in self.slots()]

    def upward(self):
        pairs = []
        for p, rho, h in self.slots():
            q, sigma = (p, rho + 1) if rho + 1 < SLOTS else (p + 1, 0)
            if q < self.pairs:
                pairs.append((self.place(p, rho, h), self.place(q, sigma, h)))
        return pairs


def after(x, *others):
    return lax.optimization_barrier((x,) + others)[0]


def flipped(pairs):
    return [(b, a) for a, b in pairs]


def tables(length, modes, lon, share):
    n = np.arange(length)
    m = np.arange(modes)
    angle = (n[:, None] * m[None, :] % length) * (2.0 * math.pi / length)
    root = np.sqrt(np.where(m == 0, 1.0, 2.0) / length)
    part_len, width = length // lon, modes // share
    wide = -(-width // 16) * 16
    parts = np.stack([(f * root).reshape(lon, part_len, share, width) for f in (np.cos(angle), -np.sin(angle))])
    out = np.zeros((share, 2, 2 * share, wide, 2 * wide), np.float32)
    for h in range(share):
        for g in range(share):
            for b in range(2):
                for half in range(2):
                    block = parts[half, b * share + (h ^ g), :, h]
                    out[h, 0, half * share + g, :width, b * part_len : (b + 1) * part_len] = block.T
                    out[h, 1, 2 * g + b, :part_len, half * wide : half * wide + width] = block
    return np.stack(split(out)), wide


def split(x):
    high = x.astype(BF16)
    return high, (x - high.astype(np.float32)).astype(BF16)


def split_outside(x):
    high = lax.reduce_precision(x, 8, 7)
    return high.astype(BF16), (x - high).astype(BF16)


def dot3(a, b, dims=(((1,), (0,)), ((), ()))):
    out = lax.dot_general(a[0], b[0], dims, preferred_element_type=jnp.float32)
    out += lax.dot_general(a[0], b[1], dims, preferred_element_type=jnp.float32)
    return out + lax.dot_general(a[1], b[0], dims, preferred_element_type=jnp.float32)


WHOLE = pl.BlockSpec(memory_space=pltpu.VMEM)
REMAIN = pl.BlockSpec(memory_space=pltpu.HBM)
CHEAP = pl.CostEstimate(flops=1, bytes_accessed=1, transcendentals=0)


def kernel_call(body, grid, in_specs, out_specs, out_shape, scratch=()):
    return pl.pallas_call(
        body,
        grid_spec=pltpu.PrefetchScalarGridSpec(
            num_scalar_prefetch=1, grid=grid, in_specs=in_specs, out_specs=out_specs, scratch_shapes=list(scratch)
        ),
        out_shape=out_shape,
        compiler_params=pltpu.CompilerParams(vmem_limit_bytes=VMEM),
        cost_estimate=CHEAP,
    )


def copies(table, blocks, buffers, sems):
    started = []
    for i, block in enumerate(blocks):
        pair = [pltpu.make_async_copy(table.at[(term, *block)], buffers.at[term, i], sems.at[term, i]) for term in range(2)]
        for copy in pair:
            copy.start()
        started.append(pair)
    return started


def fetched(refs, buffer, sems):
    started = [pltpu.make_async_copy(ref, buffer.at[i], sems.at[i]) for i, ref in enumerate(refs)]
    for copy in started:
        copy.start()
    return started


def arrived(pair):
    for copy in pair:
        copy.wait()


def transform(place, blocks, table):
    share, wide, wide2 = table.shape[1], *table.shape[-2:]
    channels = blocks[0].shape[-1]
    count = len(blocks)

    def body(place, *refs):
        ins, (table, out, x, v, sems, held, held_sems) = refs[:count], refs[count:]
        loads = fetched(ins, held, held_sems)
        pairs = copies(table, [(place[0], 0, i) for i in range(2 * share)], v, sems)
        for g in range(share):
            if count == 1:
                if g == 0:
                    arrived(loads)
                x[0, g], x[1, g] = split(held[0, g])
                continue
            arrived(loads[2 * g : 2 * g + 2])
            a, b = held[2 * g], held[2 * g + 1]
            swap = place[1] == 1
            size = 2 * a.shape[0]
            pair = jnp.concatenate([jnp.where(swap, b, a), jnp.where(swap, a, b)], axis=0)
            x[0, g, :size, :], x[1, g, :size, :] = split(pair)
            for term in range(2):
                x[term, g, size:, :] = jnp.zeros((wide2 - size, channels), BF16)
        for half in range(2):
            total = 0.0
            for g in range(share):
                i = half * share + g
                arrived(pairs[i])
                total += dot3((v[0, i], v[1, i]), (x[0, g], x[1, g]))
            out[half * wide : (half + 1) * wide, :] = total

    return kernel_call(
        body,
        (),
        [REMAIN] * (count + 1),
        WHOLE,
        jax.ShapeDtypeStruct((wide2, channels), jnp.float32),
        [
            pltpu.VMEM((2, share, wide2, channels), BF16),
            pltpu.VMEM((2, 2 * share, wide, wide2), BF16),
            pltpu.SemaphoreType.DMA((2, 2 * share)),
            pltpu.VMEM((count, *blocks[0].shape), jnp.float32),
            pltpu.SemaphoreType.DMA((count,)),
        ],
    )(place, *blocks, table)


def mix(place, rows, coef, weights, table, part_len, gradient=None):
    share, wide, wide2 = table.shape[1], *table.shape[-2:]
    channels = weights[0].shape[1]
    deep = weights[0].shape[0]
    basis = deep // channels
    chunk = 16
    count = 2 * share
    rows = [*rows] + ([] if gradient is None else [gradient])
    n_rows = len(rows)
    n_in = n_rows + 4

    def body(place, *refs):
        coef, wh, wl, table = refs[n_rows:n_in]
        ys, rest = refs[n_in : n_in + count], refs[n_in + count :]
        if gradient is not None:
            out, gh, gl, *rest = rest
        fh, fl, oh, ol, v, sems, held, held_sems, w, w_sems = rest
        loads = fetched(refs[:n_rows], held, held_sems)
        w_loads = fetched((wh, wl), w, w_sems)
        blocks = [(place[0], 1, 2 * (i // 2) + (place[1] ^ (i % 2))) for i in range(count)]
        pairs = copies(table, blocks, v, sems)
        arrived(loads)

        @pl.loop(0, wide // chunk)
        def _(i):
            re_at = pl.ds(pl.multiple_of(i * chunk, chunk), chunk)
            im_at = pl.ds(pl.multiple_of(wide + i * chunk, chunk), chunk)
            c = coef[re_at, :]
            data = [(held[d, re_at, :], held[d, im_at, :]) for d in range(3)]
            for k in range(basis):
                re, im = 0.0, 0.0
                for d, (xr, xi) in enumerate(data):
                    at = (d * basis + k) * 2
                    pr, pi = c[:, at : at + 1], c[:, at + 1 : at + 2]
                    re += pr * xr - pi * xi
                    im += pr * xi + pi * xr
                cols = pl.ds(k * channels, channels)
                fh[re_at, cols], fl[re_at, cols] = split(re)
                fh[im_at, cols], fl[im_at, cols] = split(im)

        arrived(w_loads)
        oh[...], ol[...] = split(dot3((fh[...], fl[...]), (w[0], w[1])))
        for i, y in enumerate(ys):
            arrived(pairs[i])
            y[...] = dot3((v[0, i], v[1, i]), (oh[...], ol[...]))[:part_len]
        if gradient is not None:
            gh[...], gl[...] = split(held[3])
            for k in range(basis):
                at = pl.ds(k * channels, channels)
                out[at, :] = dot3((fh[:, at], fl[:, at]), (gh[...], gl[...]), (((0,), (0,)), ((), ())))

    y_shape = jax.ShapeDtypeStruct((part_len, channels), jnp.float32)
    extra, scratch = [], []
    if gradient is not None:
        extra = [jax.ShapeDtypeStruct((deep, channels), jnp.float32)]
        scratch = [pltpu.VMEM((wide2, channels), BF16)] * 2
    return kernel_call(
        body,
        (),
        [REMAIN] * n_rows + [WHOLE] + [REMAIN] * 3,
        [WHOLE] * (count + len(extra)),
        [y_shape] * count + extra,
        scratch
        + [pltpu.VMEM((wide2, deep), BF16)] * 2
        + [pltpu.VMEM((wide2, channels), BF16)] * 2
        + [pltpu.VMEM((2, count, wide, wide2), BF16), pltpu.SemaphoreType.DMA((2, count))]
        + [pltpu.VMEM((n_rows, wide2, channels), jnp.float32), pltpu.SemaphoreType.DMA((n_rows,))]
        + [pltpu.VMEM((2, deep, channels), BF16), pltpu.SemaphoreType.DMA((2,))],
    )(place, *rows, coef, *weights, table)


def arrange(flags, got):
    part_len, channels = got[0].shape

    def body(flags, a, b, out):
        swap, full = flags[0] == 1, flags[1] == 1
        x, y = a[...], b[...]
        first, second = jnp.where(swap, y, x), jnp.where(swap, x, y)
        out[0] = jnp.where(full, first, first + second)
        out[1] = jnp.where(full, second, 0.0)

    return kernel_call(
        body,
        (),
        [WHOLE, WHOLE],
        WHOLE,
        jax.ShapeDtypeStruct((2, part_len, channels), jnp.float32),
    )(flags, *got)


def shares_sent(x, axis, me, ways, stride):
    parts = x.reshape(ways, -1, x.shape[-1])
    size = lax.axis_size(axis)
    pieces = [lax.dynamic_index_in_dim(parts, me, 0, keepdims=False)]
    for g in range(1, ways):
        piece = lax.dynamic_index_in_dim(parts, me ^ g, 0, keepdims=False)
        pieces.append(lax.ppermute(piece, axis, [(a, a ^ (g * stride)) for a in range(size)]))
    return pieces


def shares_summed(pieces):
    total = pieces[0]
    for piece in pieces[1:]:
        total = total + piece
    return total


def shares_joined(x, axis, me, ways, stride):
    size = lax.axis_size(axis)
    whole = jnp.zeros((ways,) + x.shape, x.dtype)
    whole = lax.dynamic_update_index_in_dim(whole, x, me, 0)
    for g in range(1, ways):
        piece = lax.ppermute(x, axis, [(a, a ^ (g * stride)) for a in range(size)])
        whole = lax.dynamic_update_index_in_dim(whole, piece, me ^ g, 0)
    return whole.reshape((-1,) + x.shape[1:])


def make_local(lat, lon):
    lay = Layout(lat, lon)
    share = lay.share

    def send(x, pairs):
        return lax.ppermute(x, AXES, pairs)

    def local(signal, band_rows, filter_modes, mixing, cotangent):
        channels = signal.shape[2]
        part_len = signal.shape[1]
        length = part_len * lon
        modes = filter_modes.shape[-1]
        basis = mixing.shape[0]
        width = modes // share

        band = lax.axis_index("lat")
        z = lax.axis_index("lon")
        core = band % 2
        v = jnp.where((band // 2) % 2 == 0, z, lon - 1 - z)
        rho = v // lay.chips
        h = (v % lay.chips) * 2 + core
        r_held = rho % 2
        live = lax.dynamic_index_in_dim(band_rows, band, 0, keepdims=False)
        full = live == 2
        high_z = z // share

        table, wide = tables(length, modes, lon, share)
        table = jnp.asarray(table)
        place = jnp.stack([h, r_held]).astype(jnp.int32)
        flags = jnp.stack([high_z, full.astype(jnp.int32)]).astype(jnp.int32)

        def fetch(x, then=None):
            got = []
            for t in range(2):
                row = jnp.minimum(high_z ^ t, live - 1)
                message = lax.dynamic_index_in_dim(x, row, 0, keepdims=False)
                if then is not None:
                    message = after(message, *then)
                got.append(send(message, lay.inward(t)))
            return got

        def enter(got):
            blocks = list(got)
            for g in range(1, share):
                blocks += [send(x, lay.within(g)) for x in got]
            if part_len % 8:
                pairs = []
                for x, y in zip(blocks[::2], blocks[1::2]):
                    pairs += [jnp.where(r_held == 0, x, y), jnp.where(r_held == 0, y, x)]
                blocks = jnp.concatenate(pairs, axis=0).reshape(share, 2 * part_len, channels)
                blocks = [jnp.pad(blocks, ((0, 0), (0, 2 * (wide - part_len)), (0, 0)))]
            return transform(place, blocks, table)

        def exchange(y):
            return [[send(y[2 * g + t], lay.within(g)) for t in range(2)] for g in range(1, share)]

        def total(own, others):
            return [own[t] + sum(other[t] for other in others) for t in range(2)]

        def deliver(block, t):
            return send(block, flipped(lay.inward(t)))

        def halo(spec):
            return send(spec, lay.upward()), send(spec, flipped(lay.upward()))

        s_got = fetch(signal)
        f = after(filter_modes, *s_got)
        ladder = [(i, i + 1) for i in range(lat - 1)]
        below = lax.ppermute(jnp.where(full, f[1, 2], f[0, 2]), "lat", ladder)
        above = lax.ppermute(f[0, 0], "lat", flipped(ladder))
        nil = jnp.zeros_like(below)
        is_first = r_held == 0
        ahead = [
            jnp.where(is_first, f[0, 0], jnp.where(full, f[1, 0], nil)),
            jnp.where(is_first, f[0, 1], jnp.where(full, f[1, 1], nil)),
            jnp.where(is_first, jnp.where(full, f[0, 2], nil), jnp.where(full, f[1, 2], f[0, 2])),
        ]
        back = [
            jnp.where(is_first, below, jnp.where(full, f[0, 2], nil)),
            jnp.where(is_first, f[0, 1], jnp.where(full, f[1, 1], nil)),
            jnp.where(is_first, jnp.where(full, f[1, 0], nil), above),
        ]
        conj = jnp.array([1.0, -1.0], jnp.float32)[None, None, :, None]
        both = jnp.stack([jnp.stack(ahead), jnp.stack(back) * conj])
        both = both.reshape(2 * 3 * basis * 2, modes)
        swap = [(i, i ^ 1) for i in range(lat)]
        theirs = lax.ppermute(lax.dynamic_slice_in_dim(both, (h ^ 1) * width, width, 1), "lat", swap)
        mine = lax.dynamic_slice_in_dim(both, h * width, width, 1)
        coef = jnp.where(rho // 2 == core, mine, theirs).reshape(2, 3 * basis * 2, width)
        coef = jnp.pad(jnp.transpose(coef, (0, 2, 1)), ((0, 0), (0, wide - width), (0, 0)))

        flat = (basis * channels, channels)
        ahead_weights = split_outside(mixing.reshape(flat))
        back_weights = split_outside(jnp.transpose(mixing, (0, 2, 1)).reshape(flat))

        pair = band // 2
        even = (basis * channels // lat) * channels % (lon * 128) == 0

        def swap_core(x):
            return lax.ppermute(x, "lat", swap)

        s_got = [after(x, *ahead_weights, *back_weights) for x in s_got]
        g_got = fetch(cotangent, s_got)
        s_spec = enter(s_got)
        g_got = [after(x, s_spec, coef) for x in g_got]
        s_halo = halo(after(s_spec, *g_got))
        g_spec = enter(g_got)
        s_halo = [after(x, g_spec) for x in s_halo]
        g_halo = halo(g_spec)
        *y, term = mix(place, (s_halo[0], s_spec, s_halo[1]), coef[0], ahead_weights, table, part_len, g_spec)
        g_halo = [after(x, *y) for x in g_halo]
        others = exchange([after(x, *g_halo) for x in y])
        halves = term.reshape(2, -1, channels)
        give = after(lax.dynamic_index_in_dim(halves, 1 - core, 0, keepdims=False), *g_halo)
        given = swap_core(give)
        o_blocks = total(y, others)

        o_got = [deliver(x, t) for t, x in enumerate(o_blocks)]
        term = lax.dynamic_index_in_dim(halves, core, 0, keepdims=False) + after(given, *o_blocks)
        pieces = shares_sent(term, "lat", pair, lay.pairs, 2)
        g_halo = [after(x, *o_blocks, term) for x in g_halo]
        y = mix(place, (g_halo[0], g_spec, g_halo[1]), coef[1], back_weights, table, part_len)
        o_got = [after(x, *y) for x in o_got]
        y = [after(x, *o_got) for x in y]
        others = exchange(y)
        term = shares_summed([after(x, *o_got) for x in pieces])
        term_shape = term.shape
        term = term.reshape((-1, 128) if even else (lon, -1))
        pieces = shares_sent(term, "lon", z, lon, 1)
        b_blocks = total(y, others)
        term = shares_summed([after(x, *b_blocks) for x in pieces])
        b_got = [deliver(after(x, term), t) for t, x in enumerate(b_blocks)]
        term = shares_joined(term, "lon", z, lon, 1).reshape(term_shape)
        output = arrange(flags, o_got)
        b_got = [after(x, output) for x in b_got]
        term = shares_joined(term, "lat", pair, lay.pairs, 2)
        b_got = [after(x, term) for x in b_got]
        other = swap_core(after(term, *b_got))
        grad_signal = arrange(flags, b_got)
        term = jnp.concatenate([jnp.where(core == 0, term, other), jnp.where(core == 0, other, term)], axis=0)
        weight_grad = term.reshape(mixing.shape)
        return output, grad_signal, weight_grad

    return local


def solution(mesh):
    lat, lon = mesh.shape["lat"], mesh.shape["lon"]
    grid = P("lat", "lon", None)
    return jax.shard_map(
        make_local(lat, lon),
        mesh=mesh,
        in_specs=(grid, P(), P("lat", None, None, None, None), P(), grid),
        out_specs=(grid, grid, P()),
        check_vma=False,
    )
```

```python
import math

import jax
import jax.numpy as jnp
import numpy as np
from jax import lax
from jax.experimental import pallas as pl
from jax.experimental.pallas import tpu as pltpu
from jax.sharding import PartitionSpec as P

AXES = ("lat", "lon")
SLOTS = 4
VMEM = 48 * 2**20
BF16 = jnp.bfloat16


class Layout:
    def __init__(self, lat, lon):
        self.lat, self.lon, self.pairs = lat, lon, lat // 2
        self.chips = lon // SLOTS
        self.share = 2 * self.chips

    def device(self, band, z):
        return band * self.lon + z

    def place(self, pair, rho, h):
        v = rho * self.chips + h // 2
        z = v if pair % 2 == 0 else self.lon - 1 - v
        return self.device(2 * pair + h % 2, z)

    def inward(self, t):
        pairs = []
        for band in range(self.lat):
            for z in range(self.lon):
                r = (z // self.share) ^ t
                dst = self.place(band // 2, 2 * (band % 2) + r, z % self.share)
                pairs.append((self.device(band, z), dst))
        return pairs

    def slots(self):
        for pair in range(self.pairs):
            for rho in range(SLOTS):
                for h in range(self.share):
                    yield pair, rho, h

    def within(self, g):
        return [(self.place(p, rho, h), self.place(p, rho, h ^ g)) for p, rho, h in self.slots()]

    def upward(self):
        pairs = []
        for p, rho, h in self.slots():
            q, sigma = (p, rho + 1) if rho + 1 < SLOTS else (p + 1, 0)
            if q < self.pairs:
                pairs.append((self.place(p, rho, h), self.place(q, sigma, h)))
        return pairs


def after(x, *others):
    return lax.optimization_barrier((x,) + others)[0]


def flipped(pairs):
    return [(b, a) for a, b in pairs]


def tables(length, modes, lon, share):
    n = np.arange(length)
    m = np.arange(modes)
    angle = (n[:, None] * m[None, :] % length) * (2.0 * math.pi / length)
    root = np.sqrt(np.where(m == 0, 1.0, 2.0) / length)
    part_len, width = length // lon, modes // share
    wide = -(-width // 16) * 16
    parts = np.stack([(f * root).reshape(lon, part_len, share, width) for f in (np.cos(angle), -np.sin(angle))])
    out = np.zeros((share, 2, 2 * share, wide, 2 * wide), np.float32)
    for h in range(share):
        for g in range(share):
            for b in range(2):
                for half in range(2):
                    block = parts[half, b * share + (h ^ g), :, h]
                    out[h, 0, half * share + g, :width, b * part_len : (b + 1) * part_len] = block.T
                    out[h, 1, 2 * g + b, :part_len, half * wide : half * wide + width] = block
    return np.stack(split(out)), wide


def split(x):
    high = x.astype(BF16)
    return high, (x - high.astype(np.float32)).astype(BF16)


def split_outside(x):
    high = lax.reduce_precision(x, 8, 7)
    return jnp.concatenate([high.astype(BF16), (x - high).astype(BF16)], axis=1)


def dot3(a, b, dims=(((1,), (0,)), ((), ()))):
    columns = b.shape[1] // 2
    both = lax.dot_general(a[0], b, dims, preferred_element_type=jnp.float32)
    rest = lax.dot_general(a[1], b[:, :columns], dims, preferred_element_type=jnp.float32)
    return both[:, :columns] + both[:, columns:] + rest


def side_by_side(x):
    return jnp.concatenate(split(x), axis=1)


WHOLE = pl.BlockSpec(memory_space=pltpu.VMEM)
REMAIN = pl.BlockSpec(memory_space=pltpu.HBM)
CHEAP = pl.CostEstimate(flops=1, bytes_accessed=1, transcendentals=0)


def kernel_call(body, grid, in_specs, out_specs, out_shape, scratch=()):
    return pl.pallas_call(
        body,
        grid_spec=pltpu.PrefetchScalarGridSpec(
            num_scalar_prefetch=1, grid=grid, in_specs=in_specs, out_specs=out_specs, scratch_shapes=list(scratch)
        ),
        out_shape=out_shape,
        compiler_params=pltpu.CompilerParams(vmem_limit_bytes=VMEM),
        cost_estimate=CHEAP,
    )


def copies(table, blocks, buffers, sems):
    started = []
    for i, block in enumerate(blocks):
        pair = [pltpu.make_async_copy(table.at[(term, *block)], buffers.at[term, i], sems.at[term, i]) for term in range(2)]
        for copy in pair:
            copy.start()
        started.append(pair)
    return started


def fetched(refs, buffer, sems):
    started = [pltpu.make_async_copy(ref, buffer.at[i], sems.at[i]) for i, ref in enumerate(refs)]
    for copy in started:
        copy.start()
    return started


def arrived(pair):
    for copy in pair:
        copy.wait()


def transform(place, blocks, table):
    share, wide, wide2 = table.shape[1], *table.shape[-2:]
    channels = blocks[0].shape[-1]
    count = len(blocks)

    def body(place, *refs):
        ins, (table, out, x, v, sems, held, held_sems) = refs[:count], refs[count:]
        loads = fetched(ins, held, held_sems)
        pairs = copies(table, [(place[0], 0, i) for i in range(2 * share)], v, sems)
        for g in range(share):
            if count == 1:
                if g == 0:
                    arrived(loads)
                x[g] = side_by_side(held[0, g])
                continue
            arrived(loads[2 * g : 2 * g + 2])
            a, b = held[2 * g], held[2 * g + 1]
            swap = place[1] == 1
            size = 2 * a.shape[0]
            pair = jnp.concatenate([jnp.where(swap, b, a), jnp.where(swap, a, b)], axis=0)
            x[g, :size, :] = side_by_side(pair)
            x[g, size:, :] = jnp.zeros((wide2 - size, 2 * channels), BF16)
        for half in range(2):
            total = 0.0
            for g in range(share):
                i = half * share + g
                arrived(pairs[i])
                total += dot3((v[0, i], v[1, i]), x[g])
            out[half * wide : (half + 1) * wide, :] = total

    return kernel_call(
        body,
        (),
        [REMAIN] * (count + 1),
        WHOLE,
        jax.ShapeDtypeStruct((wide2, channels), jnp.float32),
        [
            pltpu.VMEM((share, wide2, 2 * channels), BF16),
            pltpu.VMEM((2, 2 * share, wide, wide2), BF16),
            pltpu.SemaphoreType.DMA((2, 2 * share)),
            pltpu.VMEM((count, *blocks[0].shape), jnp.float32),
            pltpu.SemaphoreType.DMA((count,)),
        ],
    )(place, *blocks, table)


def mix(place, rows, coef, weights, table, part_len, gradient=None):
    share, wide, wide2 = table.shape[1], *table.shape[-2:]
    deep, channels = weights.shape[0], weights.shape[1] // 2
    basis = deep // channels
    chunk = 16
    count = 2 * share
    rows = [*rows] + ([] if gradient is None else [gradient])
    n_rows = len(rows)
    n_in = n_rows + 3

    def body(place, *refs):
        coef, weights, table = refs[n_rows:n_in]
        ys, rest = refs[n_in : n_in + count], refs[n_in + count :]
        if gradient is not None:
            out, both, *rest = rest
        fh, fl, mixed, v, sems, held, held_sems, w, w_sems = rest
        loads = fetched(refs[:n_rows], held, held_sems)
        arrived(loads)
        w_loads = fetched((weights,), w, w_sems)
        blocks = [(place[0], 1, 2 * (i // 2) + (place[1] ^ (i % 2))) for i in range(count)]
        pairs = copies(table, blocks, v, sems)

        @pl.loop(0, wide // chunk, unroll=True)
        def _(i):
            re_at = pl.ds(pl.multiple_of(i * chunk, chunk), chunk)
            im_at = pl.ds(pl.multiple_of(wide + i * chunk, chunk), chunk)
            c = coef[re_at, :]
            data = [(held[d, re_at, :], held[d, im_at, :]) for d in range(3)]
            for k in range(basis):
                re, im = 0.0, 0.0
                for d, (xr, xi) in enumerate(data):
                    at = (d * basis + k) * 2
                    pr, pi = c[:, at : at + 1], c[:, at + 1 : at + 2]
                    re += pr * xr - pi * xi
                    im += pr * xi + pi * xr
                cols = pl.ds(k * channels, channels)
                fh[re_at, cols], fl[re_at, cols] = split(re)
                fh[im_at, cols], fl[im_at, cols] = split(im)

        arrived(w_loads)
        mixed[...] = side_by_side(dot3((fh[...], fl[...]), w[0]))
        for i, y in enumerate(ys):
            arrived(pairs[i])
            y[...] = dot3((v[0, i], v[1, i]), mixed[...])[:part_len]
        if gradient is not None:
            both[...] = side_by_side(held[3])
            for k in range(basis):
                at = pl.ds(k * channels, channels)
                out[at, :] = dot3((fh[:, at], fl[:, at]), both[...], (((0,), (0,)), ((), ())))

    y_shape = jax.ShapeDtypeStruct((part_len, channels), jnp.float32)
    extra, scratch = [], []
    if gradient is not None:
        extra = [jax.ShapeDtypeStruct((deep, channels), jnp.float32)]
        scratch = [pltpu.VMEM((wide2, 2 * channels), BF16)]
    return kernel_call(
        body,
        (),
        [REMAIN] * n_rows + [WHOLE] + [REMAIN] * 2,
        [WHOLE] * (count + len(extra)),
        [y_shape] * count + extra,
        scratch
        + [pltpu.VMEM((wide2, deep), BF16)] * 2
        + [pltpu.VMEM((wide2, 2 * channels), BF16)]
        + [pltpu.VMEM((2, count, wide, wide2), BF16), pltpu.SemaphoreType.DMA((2, count))]
        + [pltpu.VMEM((n_rows, wide2, channels), jnp.float32), pltpu.SemaphoreType.DMA((n_rows,))]
        + [pltpu.VMEM((1, deep, 2 * channels), BF16), pltpu.SemaphoreType.DMA((1,))],
    )(place, *rows, coef, weights, table)


def arrange(flags, got):
    part_len, channels = got[0].shape

    def body(flags, a, b, out):
        swap, full = flags[0] == 1, flags[1] == 1
        x, y = a[...], b[...]
        first, second = jnp.where(swap, y, x), jnp.where(swap, x, y)
        out[0] = jnp.where(full, first, first + second)
        out[1] = jnp.where(full, second, 0.0)

    return kernel_call(
        body,
        (),
        [WHOLE, WHOLE],
        WHOLE,
        jax.ShapeDtypeStruct((2, part_len, channels), jnp.float32),
    )(flags, *got)


def shares_sent(x, axis, me, ways, stride):
    parts = x.reshape(ways, -1, x.shape[-1])
    size = lax.axis_size(axis)
    pieces = [lax.dynamic_index_in_dim(parts, me, 0, keepdims=False)]
    for g in range(1, ways):
        piece = lax.dynamic_index_in_dim(parts, me ^ g, 0, keepdims=False)
        pieces.append(lax.ppermute(piece, axis, [(a, a ^ (g * stride)) for a in range(size)]))
    return pieces


def shares_summed(pieces):
    total = pieces[0]
    for piece in pieces[1:]:
        total = total + piece
    return total


def share_shown(x, axis, ways, stride):
    size = lax.axis_size(axis)
    return [x] + [lax.ppermute(x, axis, [(a, a ^ (g * stride)) for a in range(size)]) for g in range(1, ways)]


def shares_joined(pieces, me):
    ways = len(pieces)
    whole = jnp.zeros((ways,) + pieces[0].shape, pieces[0].dtype)
    for g, piece in enumerate(pieces):
        whole = lax.dynamic_update_index_in_dim(whole, piece, me ^ g, 0)
    return whole.reshape((-1,) + pieces[0].shape[1:])


def make_local(lat, lon):
    lay = Layout(lat, lon)
    share = lay.share

    def send(x, pairs):
        return lax.ppermute(x, AXES, pairs)

    def local(signal, band_rows, filter_modes, mixing, cotangent):
        channels = signal.shape[2]
        part_len = signal.shape[1]
        length = part_len * lon
        modes = filter_modes.shape[-1]
        basis = mixing.shape[0]
        width = modes // share

        band = lax.axis_index("lat")
        z = lax.axis_index("lon")
        core = band % 2
        v = jnp.where((band // 2) % 2 == 0, z, lon - 1 - z)
        rho = v // lay.chips
        h = (v % lay.chips) * 2 + core
        r_held = rho % 2
        live = lax.dynamic_index_in_dim(band_rows, band, 0, keepdims=False)
        full = live == 2
        high_z = z // share

        table, wide = tables(length, modes, lon, share)
        table = jnp.asarray(table)
        place = jnp.stack([h, r_held]).astype(jnp.int32)
        flags = jnp.stack([high_z, full.astype(jnp.int32)]).astype(jnp.int32)

        def fetch(x, then=None):
            got = []
            for t in range(2):
                row = jnp.minimum(high_z ^ t, live - 1)
                message = lax.dynamic_index_in_dim(x, row, 0, keepdims=False)
                if then is not None:
                    message = after(message, *then)
                got.append(send(message, lay.inward(t)))
            return got

        def enter(got):
            blocks = list(got)
            for g in range(1, share):
                blocks += [send(x, lay.within(g)) for x in got]
            if part_len % 8:
                pairs = []
                for x, y in zip(blocks[::2], blocks[1::2]):
                    pairs += [jnp.where(r_held == 0, x, y), jnp.where(r_held == 0, y, x)]
                blocks = jnp.concatenate(pairs, axis=0).reshape(share, 2 * part_len, channels)
                blocks = [jnp.pad(blocks, ((0, 0), (0, 2 * (wide - part_len)), (0, 0)))]
            return transform(place, blocks, table)

        def exchange(y):
            return [[send(y[2 * g + t], lay.within(g)) for t in range(2)] for g in range(1, share)]

        def total(own, others):
            return [own[t] + sum(other[t] for other in others) for t in range(2)]

        def deliver(block, t):
            return send(block, flipped(lay.inward(t)))

        def halo(spec):
            return send(spec, lay.upward()), send(spec, flipped(lay.upward()))

        s_got = fetch(signal)
        f = after(filter_modes, *s_got)
        ladder = [(i, i + 1) for i in range(lat - 1)]
        below = lax.ppermute(jnp.where(full, f[1, 2], f[0, 2]), "lat", ladder)
        above = lax.ppermute(f[0, 0], "lat", flipped(ladder))
        nil = jnp.zeros_like(below)
        is_first = r_held == 0
        ahead = [
            jnp.where(is_first, f[0, 0], jnp.where(full, f[1, 0], nil)),
            jnp.where(is_first, f[0, 1], jnp.where(full, f[1, 1], nil)),
            jnp.where(is_first, jnp.where(full, f[0, 2], nil), jnp.where(full, f[1, 2], f[0, 2])),
        ]
        back = [
            jnp.where(is_first, below, jnp.where(full, f[0, 2], nil)),
            jnp.where(is_first, f[0, 1], jnp.where(full, f[1, 1], nil)),
            jnp.where(is_first, jnp.where(full, f[1, 0], nil), above),
        ]
        conj = jnp.array([1.0, -1.0], jnp.float32)[None, None, :, None]
        both = jnp.stack([jnp.stack(ahead), jnp.stack(back) * conj])
        both = both.reshape(2 * 3 * basis * 2, modes)
        swap = [(i, i ^ 1) for i in range(lat)]
        theirs = lax.ppermute(lax.dynamic_slice_in_dim(both, (h ^ 1) * width, width, 1), "lat", swap)
        mine = lax.dynamic_slice_in_dim(both, h * width, width, 1)
        coef = jnp.where(rho // 2 == core, mine, theirs).reshape(2, 3 * basis * 2, width)
        coef = jnp.pad(jnp.transpose(coef, (0, 2, 1)), ((0, 0), (0, wide - width), (0, 0)))

        flat = (basis * channels, channels)
        ahead_weights = split_outside(mixing.reshape(flat))
        back_weights = split_outside(jnp.transpose(mixing, (0, 2, 1)).reshape(flat))

        pair = band // 2
        even = (basis * channels // lat) * channels % (lon * 128) == 0

        def swap_core(x):
            return lax.ppermute(x, "lat", swap)

        s_got = [after(x, ahead_weights, back_weights) for x in s_got]
        g_got = fetch(cotangent, s_got)
        s_spec = enter(s_got)
        g_got = [after(x, s_spec, coef) for x in g_got]
        s_halo = halo(s_spec)
        g_spec = enter(g_got)
        s_halo = [after(x, g_spec) for x in s_halo]
        g_halo = halo(g_spec)
        *y, term = mix(place, (s_halo[0], s_spec, s_halo[1]), coef[0], ahead_weights, table, part_len, g_spec)
        g_halo = [after(x, *y) for x in g_halo]
        others = [[after(x, *g_halo) for x in other] for other in exchange(y)]
        halves = term.reshape(2, -1, channels)
        give = after(lax.dynamic_index_in_dim(halves, 1 - core, 0, keepdims=False), *g_halo)
        given = swap_core(give)
        o_blocks = total(y, others)

        o_got = [deliver(x, t) for t, x in enumerate(o_blocks)]
        term = lax.dynamic_index_in_dim(halves, core, 0, keepdims=False) + after(given, *o_blocks)
        pieces = shares_sent(term, "lat", pair, lay.pairs, 2)
        g_halo = [after(x, *o_blocks, term) for x in g_halo]
        y = mix(place, (g_halo[0], g_spec, g_halo[1]), coef[1], back_weights, table, part_len)
        o_got = [after(x, *y) for x in o_got]
        y = [after(x, o_got[0]) for x in y]
        others = [[after(x, *o_got) for x in other] for other in exchange(y)]
        term = shares_summed([after(x, *y) for x in pieces])
        term_shape = term.shape
        term = term.reshape((-1, 128) if even else (lon, -1))
        pieces = shares_sent(term, "lon", z, lon, 1)
        b_blocks = total(y, others)
        term = shares_summed([after(x, *b_blocks) for x in pieces])
        b_got = [deliver(after(x, term), t) for t, x in enumerate(b_blocks)]
        term = shares_joined(share_shown(term, "lon", lon, 1), z).reshape(term_shape)
        output = arrange(flags, o_got)
        b_got = [after(x, output) for x in b_got]
        term = shares_joined([after(x, b_got[0]) for x in share_shown(term, "lat", lay.pairs, 2)], pair)
        b_got[1] = after(b_got[1], term)
        other = swap_core(after(term, b_got[1]))
        grad_signal = arrange(flags, b_got)
        term = jnp.concatenate([jnp.where(core == 0, term, other), jnp.where(core == 0, other, term)], axis=0)
        weight_grad = term.reshape(mixing.shape)
        return output, grad_signal, weight_grad

    return local


def solution(mesh):
    lat, lon = mesh.shape["lat"], mesh.shape["lon"]
    grid = P("lat", "lon", None)
    return jax.shard_map(
        make_local(lat, lon),
        mesh=mesh,
        in_specs=(grid, P(), P("lat", None, None, None, None), P(), grid),
        out_specs=(grid, grid, P()),
        check_vma=False,
    )
```

```python
import math

import jax
import jax.numpy as jnp
import numpy as np
from jax import lax
from jax.experimental import pallas as pl
from jax.experimental.pallas import tpu as pltpu
from jax.sharding import PartitionSpec as P

AXES = ("lat", "lon")
SLOTS = 4
VMEM = 48 * 2**20
BF16 = jnp.bfloat16


class Layout:
    def __init__(self, lat, lon):
        self.lat, self.lon, self.pairs = lat, lon, lat // 2
        self.chips = lon // SLOTS
        self.share = 2 * self.chips

    def device(self, band, z):
        return band * self.lon + z

    def place(self, pair, rho, h):
        v = rho * self.chips + h // 2
        z = v if pair % 2 == 0 else self.lon - 1 - v
        return self.device(2 * pair + h % 2, z)

    def inward(self, t):
        pairs = []
        for band in range(self.lat):
            for z in range(self.lon):
                r = (z // self.share) ^ t
                dst = self.place(band // 2, 2 * (band % 2) + r, z % self.share)
                pairs.append((self.device(band, z), dst))
        return pairs

    def slots(self):
        for pair in range(self.pairs):
            for rho in range(SLOTS):
                for h in range(self.share):
                    yield pair, rho, h

    def within(self, g):
        return [(self.place(p, rho, h), self.place(p, rho, h ^ g)) for p, rho, h in self.slots()]

    def upward(self):
        pairs = []
        for p, rho, h in self.slots():
            q, sigma = (p, rho + 1) if rho + 1 < SLOTS else (p + 1, 0)
            if q < self.pairs:
                pairs.append((self.place(p, rho, h), self.place(q, sigma, h)))
        return pairs


def after(x, *others):
    return lax.optimization_barrier((x,) + others)[0]


def flipped(pairs):
    return [(b, a) for a, b in pairs]


def tables(length, modes, lon, share):
    n = np.arange(length)
    m = np.arange(modes)
    angle = (n[:, None] * m[None, :] % length) * (2.0 * math.pi / length)
    root = np.sqrt(np.where(m == 0, 1.0, 2.0) / length)
    part_len, width = length // lon, modes // share
    wide = -(-width // 16) * 16
    parts = np.stack([(f * root).reshape(lon, part_len, share, width) for f in (np.cos(angle), -np.sin(angle))])
    out = np.zeros((share, 2, 2 * share, wide, 2 * wide), np.float32)
    for h in range(share):
        for g in range(share):
            for b in range(2):
                for half in range(2):
                    block = parts[half, b * share + (h ^ g), :, h]
                    out[h, 0, half * share + g, :width, b * part_len : (b + 1) * part_len] = block.T
                    out[h, 1, 2 * g + b, :part_len, half * wide : half * wide + width] = block
    return np.stack(split(out)), wide


def split(x):
    high = x.astype(BF16)
    return high, (x - high.astype(np.float32)).astype(BF16)


def split_outside(x):
    high = lax.reduce_precision(x, 8, 7)
    return jnp.concatenate([high.astype(BF16), (x - high).astype(BF16)], axis=1)


def dot3(a, b, dims=(((1,), (0,)), ((), ()))):
    columns = b.shape[1] // 2
    both = lax.dot_general(a[0], b, dims, preferred_element_type=jnp.float32)
    rest = lax.dot_general(a[1], b[:, :columns], dims, preferred_element_type=jnp.float32)
    return both[:, :columns] + both[:, columns:] + rest


def side_by_side(x):
    return jnp.concatenate(split(x), axis=1)


WHOLE = pl.BlockSpec(memory_space=pltpu.VMEM)
REMAIN = pl.BlockSpec(memory_space=pltpu.HBM)
CHEAP = pl.CostEstimate(flops=1, bytes_accessed=1, transcendentals=0)


def kernel_call(body, grid, in_specs, out_specs, out_shape, scratch=()):
    return pl.pallas_call(
        body,
        grid_spec=pltpu.PrefetchScalarGridSpec(
            num_scalar_prefetch=1, grid=grid, in_specs=in_specs, out_specs=out_specs, scratch_shapes=list(scratch)
        ),
        out_shape=out_shape,
        compiler_params=pltpu.CompilerParams(vmem_limit_bytes=VMEM),
        cost_estimate=CHEAP,
    )


def copies(table, blocks, buffers, sems):
    started = []
    for i, block in enumerate(blocks):
        pair = [pltpu.make_async_copy(table.at[(term, *block)], buffers.at[term, i], sems.at[term, i]) for term in range(2)]
        for copy in pair:
            copy.start()
        started.append(pair)
    return started


def fetched(refs, buffer, sems):
    started = [pltpu.make_async_copy(ref, buffer.at[i], sems.at[i]) for i, ref in enumerate(refs)]
    for copy in started:
        copy.start()
    return started


def arrived(pair):
    for copy in pair:
        copy.wait()


def transform(place, blocks, table):
    share, wide, wide2 = table.shape[1], *table.shape[-2:]
    channels = blocks[0].shape[-1]
    count = len(blocks)

    def body(place, *refs):
        ins, (table, out, x, v, sems, held, held_sems) = refs[:count], refs[count:]
        loads = fetched(ins, held, held_sems)
        pairs = copies(table, [(place[0], 0, i) for i in range(2 * share)], v, sems)
        for g in range(share):
            if count == 1:
                if g == 0:
                    arrived(loads)
                x[g] = side_by_side(held[0, g])
                continue
            arrived(loads[2 * g : 2 * g + 2])
            a, b = held[2 * g], held[2 * g + 1]
            swap = place[1] == 1
            size = 2 * a.shape[0]
            pair = jnp.concatenate([jnp.where(swap, b, a), jnp.where(swap, a, b)], axis=0)
            x[g, :size, :] = side_by_side(pair)
            x[g, size:, :] = jnp.zeros((wide2 - size, 2 * channels), BF16)
        for half in range(2):
            total = 0.0
            for g in range(share):
                i = half * share + g
                arrived(pairs[i])
                total += dot3((v[0, i], v[1, i]), x[g])
            out[half * wide : (half + 1) * wide, :] = total

    return kernel_call(
        body,
        (),
        [REMAIN] * (count + 1),
        WHOLE,
        jax.ShapeDtypeStruct((wide2, channels), jnp.float32),
        [
            pltpu.VMEM((share, wide2, 2 * channels), BF16),
            pltpu.VMEM((2, 2 * share, wide, wide2), BF16),
            pltpu.SemaphoreType.DMA((2, 2 * share)),
            pltpu.VMEM((count, *blocks[0].shape), jnp.float32),
            pltpu.SemaphoreType.DMA((count,)),
        ],
    )(place, *blocks, table)


def mix(place, rows, coef, weights, table, part_len, gradient=None):
    share, wide, wide2 = table.shape[1], *table.shape[-2:]
    deep, channels = weights.shape[0], weights.shape[1] // 2
    basis = deep // channels
    chunk = 16
    count = 2 * share
    rows = [*rows] + ([] if gradient is None else [gradient])
    n_rows = len(rows)
    n_in = n_rows + 3

    def body(place, *refs):
        coef, weights, table = refs[n_rows:n_in]
        ys, rest = refs[n_in : n_in + count], refs[n_in + count :]
        if gradient is not None:
            out, both, *rest = rest
        fh, fl, mixed, v, sems, held, held_sems, w, w_sems = rest
        loads = fetched(refs[:n_rows], held, held_sems)
        arrived(loads)
        w_loads = fetched((weights,), w, w_sems)
        blocks = [(place[0], 1, 2 * (i // 2) + (place[1] ^ (i % 2))) for i in range(count)]
        pairs = copies(table, blocks, v, sems)

        @pl.loop(0, wide // chunk, unroll=True)
        def _(i):
            re_at = pl.ds(pl.multiple_of(i * chunk, chunk), chunk)
            im_at = pl.ds(pl.multiple_of(wide + i * chunk, chunk), chunk)
            c = coef[re_at, :]
            data = [(held[d, re_at, :], held[d, im_at, :]) for d in range(3)]
            for k in range(basis):
                re, im = 0.0, 0.0
                for d, (xr, xi) in enumerate(data):
                    at = (d * basis + k) * 2
                    pr, pi = c[:, at : at + 1], c[:, at + 1 : at + 2]
                    re += pr * xr - pi * xi
                    im += pr * xi + pi * xr
                cols = pl.ds(k * channels, channels)
                fh[re_at, cols], fl[re_at, cols] = split(re)
                fh[im_at, cols], fl[im_at, cols] = split(im)

        arrived(w_loads)
        mixed[...] = side_by_side(dot3((fh[...], fl[...]), w[0]))
        for i, y in enumerate(ys):
            arrived(pairs[i])
            y[...] = dot3((v[0, i], v[1, i]), mixed[...])[:part_len]
        if gradient is not None:
            both[...] = side_by_side(held[3])
            for k in range(basis):
                at = pl.ds(k * channels, channels)
                out[at, :] = dot3((fh[:, at], fl[:, at]), both[...], (((0,), (0,)), ((), ())))

    y_shape = jax.ShapeDtypeStruct((part_len, channels), jnp.float32)
    extra, scratch = [], []
    if gradient is not None:
        extra = [jax.ShapeDtypeStruct((deep, channels), jnp.float32)]
        scratch = [pltpu.VMEM((wide2, 2 * channels), BF16)]
    return kernel_call(
        body,
        (),
        [REMAIN] * n_rows + [WHOLE] + [REMAIN] * 2,
        [WHOLE] * (count + len(extra)),
        [y_shape] * count + extra,
        scratch
        + [pltpu.VMEM((wide2, deep), BF16)] * 2
        + [pltpu.VMEM((wide2, 2 * channels), BF16)]
        + [pltpu.VMEM((2, count, wide, wide2), BF16), pltpu.SemaphoreType.DMA((2, count))]
        + [pltpu.VMEM((n_rows, wide2, channels), jnp.float32), pltpu.SemaphoreType.DMA((n_rows,))]
        + [pltpu.VMEM((1, deep, 2 * channels), BF16), pltpu.SemaphoreType.DMA((1,))],
    )(place, *rows, coef, weights, table)


def arrange(flags, got):
    part_len, channels = got[0].shape

    def body(flags, a, b, out):
        swap, full = flags[0] == 1, flags[1] == 1
        x, y = a[...], b[...]
        first, second = jnp.where(swap, y, x), jnp.where(swap, x, y)
        out[0] = jnp.where(full, first, first + second)
        out[1] = jnp.where(full, second, 0.0)

    return kernel_call(
        body,
        (),
        [WHOLE, WHOLE],
        WHOLE,
        jax.ShapeDtypeStruct((2, part_len, channels), jnp.float32),
    )(flags, *got)


def shares_sent(x, axis, me, ways, stride):
    parts = x.reshape(ways, -1, x.shape[-1])
    size = lax.axis_size(axis)
    pieces = [lax.dynamic_index_in_dim(parts, me, 0, keepdims=False)]
    for g in range(1, ways):
        piece = lax.dynamic_index_in_dim(parts, me ^ g, 0, keepdims=False)
        pieces.append(lax.ppermute(piece, axis, [(a, a ^ (g * stride)) for a in range(size)]))
    return pieces


def shares_summed(pieces):
    total = pieces[0]
    for piece in pieces[1:]:
        total = total + piece
    return total


def share_shown(x, axis, ways, stride):
    size = lax.axis_size(axis)
    return [x] + [lax.ppermute(x, axis, [(a, a ^ (g * stride)) for a in range(size)]) for g in range(1, ways)]


def shares_joined(pieces, me):
    ways = len(pieces)
    whole = jnp.zeros((ways,) + pieces[0].shape, pieces[0].dtype)
    for g, piece in enumerate(pieces):
        whole = lax.dynamic_update_index_in_dim(whole, piece, me ^ g, 0)
    return whole.reshape((-1,) + pieces[0].shape[1:])


def make_local(lat, lon):
    lay = Layout(lat, lon)
    share = lay.share

    def send(x, pairs):
        return lax.ppermute(x, AXES, pairs)

    def local(signal, band_rows, filter_modes, mixing, cotangent):
        channels = signal.shape[2]
        part_len = signal.shape[1]
        length = part_len * lon
        modes = filter_modes.shape[-1]
        basis = mixing.shape[0]
        width = modes // share

        band = lax.axis_index("lat")
        z = lax.axis_index("lon")
        core = band % 2
        v = jnp.where((band // 2) % 2 == 0, z, lon - 1 - z)
        rho = v // lay.chips
        h = (v % lay.chips) * 2 + core
        r_held = rho % 2
        live = lax.dynamic_index_in_dim(band_rows, band, 0, keepdims=False)
        full = live == 2
        high_z = z // share

        table, wide = tables(length, modes, lon, share)
        table = jnp.asarray(table)
        place = jnp.stack([h, r_held]).astype(jnp.int32)
        flags = jnp.stack([high_z, full.astype(jnp.int32)]).astype(jnp.int32)

        def fetch(x, then=None):
            got = []
            for t in range(2):
                row = jnp.minimum(high_z ^ t, live - 1)
                message = lax.dynamic_index_in_dim(x, row, 0, keepdims=False)
                if then is not None:
                    message = after(message, *then)
                got.append(send(message, lay.inward(t)))
            return got

        def enter(got):
            blocks = list(got)
            for g in range(1, share):
                blocks += [send(x, lay.within(g)) for x in got]
            if part_len % 8:
                pairs = []
                for x, y in zip(blocks[::2], blocks[1::2]):
                    pairs += [jnp.where(r_held == 0, x, y), jnp.where(r_held == 0, y, x)]
                blocks = jnp.concatenate(pairs, axis=0).reshape(share, 2 * part_len, channels)
                blocks = [jnp.pad(blocks, ((0, 0), (0, 2 * (wide - part_len)), (0, 0)))]
            return transform(place, blocks, table)

        def exchange(y):
            return [[send(y[2 * g + t], lay.within(g)) for t in range(2)] for g in range(1, share)]

        def total(own, others):
            return [own[t] + sum(other[t] for other in others) for t in range(2)]

        def deliver(block, t):
            return send(block, flipped(lay.inward(t)))

        def halo(spec):
            return send(spec, lay.upward()), send(spec, flipped(lay.upward()))

        s_got = fetch(signal)
        f = after(filter_modes, *s_got)
        ladder = [(i, i + 1) for i in range(lat - 1)]
        below = lax.ppermute(jnp.where(full, f[1, 2], f[0, 2]), "lat", ladder)
        above = lax.ppermute(f[0, 0], "lat", flipped(ladder))
        nil = jnp.zeros_like(below)
        is_first = r_held == 0
        ahead = [
            jnp.where(is_first, f[0, 0], jnp.where(full, f[1, 0], nil)),
            jnp.where(is_first, f[0, 1], jnp.where(full, f[1, 1], nil)),
            jnp.where(is_first, jnp.where(full, f[0, 2], nil), jnp.where(full, f[1, 2], f[0, 2])),
        ]
        back = [
            jnp.where(is_first, below, jnp.where(full, f[0, 2], nil)),
            jnp.where(is_first, f[0, 1], jnp.where(full, f[1, 1], nil)),
            jnp.where(is_first, jnp.where(full, f[1, 0], nil), above),
        ]
        conj = jnp.array([1.0, -1.0], jnp.float32)[None, None, :, None]
        both = jnp.stack([jnp.stack(ahead), jnp.stack(back) * conj])
        both = both.reshape(2 * 3 * basis * 2, modes)
        swap = [(i, i ^ 1) for i in range(lat)]
        theirs = lax.ppermute(lax.dynamic_slice_in_dim(both, (h ^ 1) * width, width, 1), "lat", swap)
        mine = lax.dynamic_slice_in_dim(both, h * width, width, 1)
        coef = jnp.where(rho // 2 == core, mine, theirs).reshape(2, 3 * basis * 2, width)
        coef = jnp.pad(jnp.transpose(coef, (0, 2, 1)), ((0, 0), (0, wide - width), (0, 0)))

        flat = (basis * channels, channels)
        ahead_weights = split_outside(mixing.reshape(flat))
        back_weights = split_outside(jnp.transpose(mixing, (0, 2, 1)).reshape(flat))

        pair = band // 2
        even = (basis * channels // lat) * channels % (lon * 128) == 0

        def swap_core(x):
            return lax.ppermute(x, "lat", swap)

        s_got = [after(x, ahead_weights, back_weights) for x in s_got]
        g_got = fetch(cotangent, s_got)
        s_spec = enter(s_got)
        g_got = [after(x, s_spec, coef) for x in g_got]
        s_halo = halo(s_spec)
        g_spec = enter(g_got)
        s_halo = [after(x, g_spec) for x in s_halo]
        g_halo = halo(g_spec)
        *y, term = mix(place, (s_halo[0], s_spec, s_halo[1]), coef[0], ahead_weights, table, part_len, g_spec)
        g_halo = [after(x, *y) for x in g_halo]
        others = exchange(y)
        halves = term.reshape(2, -1, channels)
        give = after(lax.dynamic_index_in_dim(halves, 1 - core, 0, keepdims=False), *g_halo, *[x for other in others for x in other])
        given = swap_core(give)
        o_blocks = total(y, others)

        o_got = [deliver(x, t) for t, x in enumerate(o_blocks)]
        term = lax.dynamic_index_in_dim(halves, core, 0, keepdims=False) + after(given, *o_blocks)
        pieces = shares_sent(term, "lat", pair, lay.pairs, 2)
        g_halo = [after(x, *o_blocks, term) for x in g_halo]
        y = mix(place, (g_halo[0], g_spec, g_halo[1]), coef[1], back_weights, table, part_len)
        o_got = [after(x, *y) for x in o_got]
        y = [after(x, o_got[0]) for x in y]
        others = [[after(x, *o_got) for x in other] for other in exchange(y)]
        term = shares_summed([after(x, *y) for x in pieces])
        term_shape = term.shape
        term = term.reshape((-1, 128) if even else (lon, -1))
        pieces = shares_sent(term, "lon", z, lon, 1)
        b_blocks = total(y, others)
        term = shares_summed([after(x, *b_blocks) for x in pieces])
        b_got = [deliver(after(x, term), t) for t, x in enumerate(b_blocks)]
        term = shares_joined(share_shown(term, "lon", lon, 1), z).reshape(term_shape)
        output = arrange(flags, o_got)
        b_got = [after(x, output) for x in b_got]
        term = shares_joined([after(x, b_got[0]) for x in share_shown(term, "lat", lay.pairs, 2)], pair)
        b_got[1] = after(b_got[1], term)
        other = swap_core(after(term, b_got[1]))
        grad_signal = arrange(flags, b_got)
        term = jnp.concatenate([jnp.where(core == 0, term, other), jnp.where(core == 0, other, term)], axis=0)
        weight_grad = term.reshape(mixing.shape)
        return output, grad_signal, weight_grad

    return local


def solution(mesh):
    lat, lon = mesh.shape["lat"], mesh.shape["lon"]
    grid = P("lat", "lon", None)
    return jax.shard_map(
        make_local(lat, lon),
        mesh=mesh,
        in_specs=(grid, P(), P("lat", None, None, None, None), P(), grid),
        out_specs=(grid, grid, P()),
        check_vma=False,
    )
```

```python
import math

import jax
import jax.numpy as jnp
import numpy as np
from jax import lax
from jax.experimental import pallas as pl
from jax.experimental.pallas import tpu as pltpu
from jax.sharding import PartitionSpec as P

AXES = ("lat", "lon")
SLOTS = 4
VMEM = 51 * 2**20
BF16 = jnp.bfloat16


class Layout:
    def __init__(self, lat, lon):
        self.lat, self.lon, self.pairs = lat, lon, lat // 2
        self.chips = lon // SLOTS
        self.share = 2 * self.chips

    def device(self, band, z):
        return band * self.lon + z

    def place(self, pair, rho, h):
        v = rho * self.chips + h // 2
        z = v if pair % 2 == 0 else self.lon - 1 - v
        return self.device(2 * pair + h % 2, z)

    def inward(self, t):
        pairs = []
        for band in range(self.lat):
            for z in range(self.lon):
                r = (z // self.share) ^ t
                dst = self.place(band // 2, 2 * (band % 2) + r, z % self.share)
                pairs.append((self.device(band, z), dst))
        return pairs

    def slots(self):
        for pair in range(self.pairs):
            for rho in range(SLOTS):
                for h in range(self.share):
                    yield pair, rho, h

    def within(self, g):
        return [(self.place(p, rho, h), self.place(p, rho, h ^ g)) for p, rho, h in self.slots()]

    def upward(self):
        pairs = []
        for p, rho, h in self.slots():
            q, sigma = (p, rho + 1) if rho + 1 < SLOTS else (p + 1, 0)
            if q < self.pairs:
                pairs.append((self.place(p, rho, h), self.place(q, sigma, h)))
        return pairs


def after(x, *others):
    return lax.optimization_barrier((x,) + others)[0]


def flipped(pairs):
    return [(b, a) for a, b in pairs]


def tables(length, modes, lon, share):
    n = np.arange(length)
    m = np.arange(modes)
    angle = (n[:, None] * m[None, :] % length) * (2.0 * math.pi / length)
    root = np.sqrt(np.where(m == 0, 1.0, 2.0) / length)
    part_len, width = length // lon, modes // share
    wide = -(-width // 16) * 16
    parts = np.stack([(f * root).reshape(lon, part_len, share, width) for f in (np.cos(angle), -np.sin(angle))])
    out = np.zeros((share, 2, 2 * share, wide, 2 * wide), np.float32)
    for h in range(share):
        for g in range(share):
            for b in range(2):
                for half in range(2):
                    block = parts[half, b * share + (h ^ g), :, h]
                    out[h, 0, half * share + g, :width, b * part_len : (b + 1) * part_len] = block.T
                    out[h, 1, 2 * g + b, :part_len, half * wide : half * wide + width] = block
    return np.stack(split(out)), wide


def split(x):
    high = x.astype(BF16)
    return high, (x - high.astype(np.float32)).astype(BF16)


def split_outside(x):
    high = lax.reduce_precision(x, 8, 7)
    return jnp.concatenate([high.astype(BF16), (x - high).astype(BF16)], axis=1)


def dot3(a, b, dims=(((1,), (0,)), ((), ()))):
    columns = b.shape[1] // 2
    both = lax.dot_general(a[0], b, dims, preferred_element_type=jnp.float32)
    rest = lax.dot_general(a[1], b[:, :columns], dims, preferred_element_type=jnp.float32)
    return both[:, :columns] + both[:, columns:] + rest


def side_by_side(x):
    return jnp.concatenate(split(x), axis=1)


WHOLE = pl.BlockSpec(memory_space=pltpu.VMEM)
REMAIN = pl.BlockSpec(memory_space=pltpu.HBM)
CHEAP = pl.CostEstimate(flops=1, bytes_accessed=1, transcendentals=0)


def kernel_call(body, grid, in_specs, out_specs, out_shape, scratch=()):
    return pl.pallas_call(
        body,
        grid_spec=pltpu.PrefetchScalarGridSpec(
            num_scalar_prefetch=1, grid=grid, in_specs=in_specs, out_specs=out_specs, scratch_shapes=list(scratch)
        ),
        out_shape=out_shape,
        compiler_params=pltpu.CompilerParams(vmem_limit_bytes=VMEM),
        cost_estimate=CHEAP,
    )


def copies(table, blocks, buffers, sems):
    started = []
    for i, block in enumerate(blocks):
        pair = [pltpu.make_async_copy(table.at[(term, *block)], buffers.at[term, i], sems.at[term, i]) for term in range(2)]
        for copy in pair:
            copy.start()
        started.append(pair)
    return started


def fetched(refs, buffer, sems):
    started = [pltpu.make_async_copy(ref, buffer.at[i], sems.at[i]) for i, ref in enumerate(refs)]
    for copy in started:
        copy.start()
    return started


def arrived(pair):
    for copy in pair:
        copy.wait()


def transform(place, blocks, table):
    share, wide, wide2 = table.shape[1], *table.shape[-2:]
    channels = blocks[0].shape[-1]
    count = len(blocks)

    def body(place, *refs):
        ins, (table, out, x, v, sems, held, held_sems) = refs[:count], refs[count:]
        loads = fetched(ins, held, held_sems)
        pairs = copies(table, [(place[0], 0, i) for i in range(2 * share)], v, sems)
        for g in range(share):
            if count == 1:
                if g == 0:
                    arrived(loads)
                x[g] = side_by_side(held[0, g])
                continue
            arrived(loads[2 * g : 2 * g + 2])
            a, b = held[2 * g], held[2 * g + 1]
            swap = place[1] == 1
            size = 2 * a.shape[0]
            pair = jnp.concatenate([jnp.where(swap, b, a), jnp.where(swap, a, b)], axis=0)
            x[g, :size, :] = side_by_side(pair)
            x[g, size:, :] = jnp.zeros((wide2 - size, 2 * channels), BF16)
        for half in range(2):
            total = 0.0
            for g in range(share):
                i = half * share + g
                arrived(pairs[i])
                total += dot3((v[0, i], v[1, i]), x[g])
            out[half * wide : (half + 1) * wide, :] = total

    return kernel_call(
        body,
        (),
        [REMAIN] * (count + 1),
        WHOLE,
        jax.ShapeDtypeStruct((wide2, channels), jnp.float32),
        [
            pltpu.VMEM((share, wide2, 2 * channels), BF16),
            pltpu.VMEM((2, 2 * share, wide, wide2), BF16),
            pltpu.SemaphoreType.DMA((2, 2 * share)),
            pltpu.VMEM((count, *blocks[0].shape), jnp.float32),
            pltpu.SemaphoreType.DMA((count,)),
        ],
    )(place, *blocks, table)


def mix(place, rows, coef, weights, table, part_len, gradient=None):
    share, wide, wide2 = table.shape[1], *table.shape[-2:]
    deep, channels = weights.shape[0], weights.shape[1] // 2
    basis = deep // channels
    chunk = 16
    count = 2 * share
    rows = [*rows] + ([] if gradient is None else [gradient])
    n_rows = len(rows)
    n_in = n_rows + 3

    def body(place, *refs):
        coef, weights, table = refs[n_rows:n_in]
        ys, rest = refs[n_in : n_in + count], refs[n_in + count :]
        if gradient is not None:
            out, both, *rest = rest
        fh, fl, mixed, v, sems, held, held_sems, w, w_sems = rest
        loads = fetched(refs[:n_rows], held, held_sems)
        arrived(loads)
        w_loads = fetched((weights,), w, w_sems)
        blocks = [(place[0], 1, 2 * (i // 2) + (place[1] ^ (i % 2))) for i in range(count)]
        pairs = copies(table, blocks, v, sems)

        @pl.loop(0, wide // chunk, unroll=True)
        def _(i):
            re_at = pl.ds(pl.multiple_of(i * chunk, chunk), chunk)
            im_at = pl.ds(pl.multiple_of(wide + i * chunk, chunk), chunk)
            c = coef[re_at, :]
            data = [(held[d, re_at, :], held[d, im_at, :]) for d in range(3)]
            for k in range(basis):
                re, im = 0.0, 0.0
                for d, (xr, xi) in enumerate(data):
                    at = (d * basis + k) * 2
                    pr, pi = c[:, at : at + 1], c[:, at + 1 : at + 2]
                    re += pr * xr - pi * xi
                    im += pr * xi + pi * xr
                cols = pl.ds(k * channels, channels)
                fh[re_at, cols], fl[re_at, cols] = split(re)
                fh[im_at, cols], fl[im_at, cols] = split(im)

        arrived(w_loads)
        mixed[...] = side_by_side(dot3((fh[...], fl[...]), w[0]))
        for i, y in enumerate(ys):
            arrived(pairs[i])
            y[...] = dot3((v[0, i], v[1, i]), mixed[...])[:part_len]
        if gradient is not None:
            both[...] = side_by_side(held[3])
            for k in range(basis):
                at = pl.ds(k * channels, channels)
                out[at, :] = dot3((fh[:, at], fl[:, at]), both[...], (((0,), (0,)), ((), ())))

    y_shape = jax.ShapeDtypeStruct((part_len, channels), jnp.float32)
    extra, scratch = [], []
    if gradient is not None:
        extra = [jax.ShapeDtypeStruct((deep, channels), jnp.float32)]
        scratch = [pltpu.VMEM((wide2, 2 * channels), BF16)]
    return kernel_call(
        body,
        (),
        [REMAIN] * n_rows + [WHOLE] + [REMAIN] * 2,
        [WHOLE] * (count + len(extra)),
        [y_shape] * count + extra,
        scratch
        + [pltpu.VMEM((wide2, deep), BF16)] * 2
        + [pltpu.VMEM((wide2, 2 * channels), BF16)]
        + [pltpu.VMEM((2, count, wide, wide2), BF16), pltpu.SemaphoreType.DMA((2, count))]
        + [pltpu.VMEM((n_rows, wide2, channels), jnp.float32), pltpu.SemaphoreType.DMA((n_rows,))]
        + [pltpu.VMEM((1, deep, 2 * channels), BF16), pltpu.SemaphoreType.DMA((1,))],
    )(place, *rows, coef, weights, table)


def arrange(flags, got):
    part_len, channels = got[0].shape

    def body(flags, a, b, out):
        swap, full = flags[0] == 1, flags[1] == 1
        x, y = a[...], b[...]
        first, second = jnp.where(swap, y, x), jnp.where(swap, x, y)
        out[0] = jnp.where(full, first, first + second)
        out[1] = jnp.where(full, second, 0.0)

    return kernel_call(
        body,
        (),
        [WHOLE, WHOLE],
        WHOLE,
        jax.ShapeDtypeStruct((2, part_len, channels), jnp.float32),
    )(flags, *got)


def shares_sent(x, axis, me, ways, stride):
    parts = x.reshape(ways, -1, x.shape[-1])
    size = lax.axis_size(axis)
    pieces = [lax.dynamic_index_in_dim(parts, me, 0, keepdims=False)]
    for g in range(1, ways):
        piece = lax.dynamic_index_in_dim(parts, me ^ g, 0, keepdims=False)
        pieces.append(lax.ppermute(piece, axis, [(a, a ^ (g * stride)) for a in range(size)]))
    return pieces


def shares_summed(pieces):
    total = pieces[0]
    for piece in pieces[1:]:
        total = total + piece
    return total


def share_shown(x, axis, ways, stride):
    size = lax.axis_size(axis)
    return [x] + [lax.ppermute(x, axis, [(a, a ^ (g * stride)) for a in range(size)]) for g in range(1, ways)]


def shares_joined(pieces, me):
    ways = len(pieces)
    whole = jnp.zeros((ways,) + pieces[0].shape, pieces[0].dtype)
    for g, piece in enumerate(pieces):
        whole = lax.dynamic_update_index_in_dim(whole, piece, me ^ g, 0)
    return whole.reshape((-1,) + pieces[0].shape[1:])


def make_local(lat, lon):
    lay = Layout(lat, lon)
    share = lay.share

    def send(x, pairs):
        return lax.ppermute(x, AXES, pairs)

    def local(signal, band_rows, filter_modes, mixing, cotangent):
        channels = signal.shape[2]
        part_len = signal.shape[1]
        length = part_len * lon
        modes = filter_modes.shape[-1]
        basis = mixing.shape[0]
        width = modes // share

        band = lax.axis_index("lat")
        z = lax.axis_index("lon")
        core = band % 2
        v = jnp.where((band // 2) % 2 == 0, z, lon - 1 - z)
        rho = v // lay.chips
        h = (v % lay.chips) * 2 + core
        r_held = rho % 2
        live = lax.dynamic_index_in_dim(band_rows, band, 0, keepdims=False)
        full = live == 2
        high_z = z // share

        table, wide = tables(length, modes, lon, share)
        table = jnp.asarray(table)
        place = jnp.stack([h, r_held]).astype(jnp.int32)
        flags = jnp.stack([high_z, full.astype(jnp.int32)]).astype(jnp.int32)

        def fetch(x, then=None):
            got = []
            for t in range(2):
                row = jnp.minimum(high_z ^ t, live - 1)
                message = lax.dynamic_index_in_dim(x, row, 0, keepdims=False)
                if then is not None:
                    message = after(message, *then)
                got.append(send(message, lay.inward(t)))
            return got

        def enter(got):
            blocks = list(got)
            for g in range(1, share):
                blocks += [send(x, lay.within(g)) for x in got]
            if part_len % 8:
                pairs = []
                for x, y in zip(blocks[::2], blocks[1::2]):
                    pairs += [jnp.where(r_held == 0, x, y), jnp.where(r_held == 0, y, x)]
                blocks = jnp.concatenate(pairs, axis=0).reshape(share, 2 * part_len, channels)
                blocks = [jnp.pad(blocks, ((0, 0), (0, 2 * (wide - part_len)), (0, 0)))]
            return transform(place, blocks, table)

        def exchange(y):
            return [[send(y[2 * g + t], lay.within(g)) for t in range(2)] for g in range(1, share)]

        def total(own, others):
            return [own[t] + sum(other[t] for other in others) for t in range(2)]

        def deliver(block, t):
            return send(block, flipped(lay.inward(t)))

        def halo(spec):
            return send(spec, lay.upward()), send(spec, flipped(lay.upward()))

        s_got = fetch(signal)
        f = after(filter_modes, *s_got)
        ladder = [(i, i + 1) for i in range(lat - 1)]
        below = lax.ppermute(jnp.where(full, f[1, 2], f[0, 2]), "lat", ladder)
        above = lax.ppermute(f[0, 0], "lat", flipped(ladder))
        nil = jnp.zeros_like(below)
        is_first = r_held == 0
        ahead = [
            jnp.where(is_first, f[0, 0], jnp.where(full, f[1, 0], nil)),
            jnp.where(is_first, f[0, 1], jnp.where(full, f[1, 1], nil)),
            jnp.where(is_first, jnp.where(full, f[0, 2], nil), jnp.where(full, f[1, 2], f[0, 2])),
        ]
        back = [
            jnp.where(is_first, below, jnp.where(full, f[0, 2], nil)),
            jnp.where(is_first, f[0, 1], jnp.where(full, f[1, 1], nil)),
            jnp.where(is_first, jnp.where(full, f[1, 0], nil), above),
        ]
        conj = jnp.array([1.0, -1.0], jnp.float32)[None, None, :, None]
        both = jnp.stack([jnp.stack(ahead), jnp.stack(back) * conj])
        both = both.reshape(2 * 3 * basis * 2, modes)
        swap = [(i, i ^ 1) for i in range(lat)]
        theirs = lax.ppermute(lax.dynamic_slice_in_dim(both, (h ^ 1) * width, width, 1), "lat", swap)
        mine = lax.dynamic_slice_in_dim(both, h * width, width, 1)
        coef = jnp.where(rho // 2 == core, mine, theirs).reshape(2, 3 * basis * 2, width)
        coef = jnp.pad(jnp.transpose(coef, (0, 2, 1)), ((0, 0), (0, wide - width), (0, 0)))

        flat = (basis * channels, channels)
        ahead_weights = split_outside(mixing.reshape(flat))
        back_weights = split_outside(jnp.transpose(mixing, (0, 2, 1)).reshape(flat))

        pair = band // 2
        even = (basis * channels // lat) * channels % (lon * 128) == 0

        def swap_core(x):
            return lax.ppermute(x, "lat", swap)

        s_got = [after(x, ahead_weights, back_weights) for x in s_got]
        g_got = fetch(cotangent, s_got)
        s_spec = enter(s_got)
        g_got = [after(x, s_spec, coef) for x in g_got]
        s_halo = halo(s_spec)
        g_spec = enter(g_got)
        s_halo = [after(x, g_spec) for x in s_halo]
        g_halo = halo(g_spec)
        *y, term = mix(place, (s_halo[0], s_spec, s_halo[1]), coef[0], ahead_weights, table, part_len, g_spec)
        g_halo = [after(x, *y) for x in g_halo]
        others = exchange(y)
        halves = term.reshape(2, -1, channels)
        give = after(lax.dynamic_index_in_dim(halves, 1 - core, 0, keepdims=False), *g_halo, *[x for other in others for x in other])
        given = swap_core(give)
        o_blocks = total(y, others)

        o_got = [deliver(x, t) for t, x in enumerate(o_blocks)]
        term = lax.dynamic_index_in_dim(halves, core, 0, keepdims=False) + after(given, *o_blocks)
        pieces = shares_sent(term, "lat", pair, lay.pairs, 2)
        g_halo = [after(x, *o_blocks, term) for x in g_halo]
        y = mix(place, (g_halo[0], g_spec, g_halo[1]), coef[1], back_weights, table, part_len)
        o_got = [after(x, *y) for x in o_got]
        y = [after(x, o_got[0]) for x in y]
        others = [[after(x, *o_got) for x in other] for other in exchange(y)]
        term = shares_summed([after(x, *y) for x in pieces])
        term_shape = term.shape
        term = term.reshape((-1, 128) if even else (lon, -1))
        pieces = shares_sent(term, "lon", z, lon, 1)
        b_blocks = total(y, others)
        term = shares_summed([after(x, *b_blocks) for x in pieces])
        b_got = [deliver(after(x, term), t) for t, x in enumerate(b_blocks)]
        term = shares_joined(share_shown(term, "lon", lon, 1), z).reshape(term_shape)
        output = arrange(flags, o_got)
        b_got = [after(x, output) for x in b_got]
        term = shares_joined([after(x, b_got[0]) for x in share_shown(term, "lat", lay.pairs, 2)], pair)
        b_got[1] = after(b_got[1], term)
        other = swap_core(after(term, b_got[1]))
        grad_signal = arrange(flags, b_got)
        term = jnp.concatenate([jnp.where(core == 0, term, other), jnp.where(core == 0, other, term)], axis=0)
        weight_grad = term.reshape(mixing.shape)
        return output, grad_signal, weight_grad

    return local


def solution(mesh):
    lat, lon = mesh.shape["lat"], mesh.shape["lon"]
    grid = P("lat", "lon", None)
    return jax.shard_map(
        make_local(lat, lon),
        mesh=mesh,
        in_specs=(grid, P(), P("lat", None, None, None, None), P(), grid),
        out_specs=(grid, grid, P()),
        check_vma=False,
    )
```

```python
import math

import jax
import jax.numpy as jnp
import numpy as np
from jax import lax
from jax.experimental import pallas as pl
from jax.experimental.pallas import tpu as pltpu
from jax.sharding import PartitionSpec as P

AXES = ("lat", "lon")
SLOTS = 4
VMEM = 53 * 2**20
BF16 = jnp.bfloat16


class Layout:
    def __init__(self, lat, lon):
        self.lat, self.lon, self.pairs = lat, lon, lat // 2
        self.chips = lon // SLOTS
        self.share = 2 * self.chips

    def device(self, band, z):
        return band * self.lon + z

    def place(self, pair, rho, h):
        v = rho * self.chips + h // 2
        z = v if pair % 2 == 0 else self.lon - 1 - v
        return self.device(2 * pair + h % 2, z)

    def inward(self, t):
        pairs = []
        for band in range(self.lat):
            for z in range(self.lon):
                r = (z // self.share) ^ t
                dst = self.place(band // 2, 2 * (band % 2) + r, z % self.share)
                pairs.append((self.device(band, z), dst))
        return pairs

    def slots(self):
        for pair in range(self.pairs):
            for rho in range(SLOTS):
                for h in range(self.share):
                    yield pair, rho, h

    def within(self, g):
        return [(self.place(p, rho, h), self.place(p, rho, h ^ g)) for p, rho, h in self.slots()]

    def upward(self):
        pairs = []
        for p, rho, h in self.slots():
            q, sigma = (p, rho + 1) if rho + 1 < SLOTS else (p + 1, 0)
            if q < self.pairs:
                pairs.append((self.place(p, rho, h), self.place(q, sigma, h)))
        return pairs


def after(x, *others):
    return lax.optimization_barrier((x,) + others)[0]


def flipped(pairs):
    return [(b, a) for a, b in pairs]


def tables(length, modes, lon, share):
    n = np.arange(length)
    m = np.arange(modes)
    angle = (n[:, None] * m[None, :] % length) * (2.0 * math.pi / length)
    root = np.sqrt(np.where(m == 0, 1.0, 2.0) / length)
    part_len, width = length // lon, modes // share
    wide = -(-width // 16) * 16
    parts = np.stack([(f * root).reshape(lon, part_len, share, width) for f in (np.cos(angle), -np.sin(angle))])
    out = np.zeros((share, 2, 2 * share, wide, 2 * wide), np.float32)
    for h in range(share):
        for g in range(share):
            for b in range(2):
                for half in range(2):
                    block = parts[half, b * share + (h ^ g), :, h]
                    out[h, 0, half * share + g, :width, b * part_len : (b + 1) * part_len] = block.T
                    out[h, 1, 2 * g + b, :part_len, half * wide : half * wide + width] = block
    return np.stack(split(out)), wide


def split(x):
    high = x.astype(BF16)
    return high, (x - high.astype(np.float32)).astype(BF16)


def split_outside(x):
    high = lax.reduce_precision(x, 8, 7)
    return jnp.concatenate([high.astype(BF16), (x - high).astype(BF16)], axis=1)


def dot3(a, b, dims=(((1,), (0,)), ((), ()))):
    columns = b.shape[1] // 2
    both = lax.dot_general(a[0], b, dims, preferred_element_type=jnp.float32)
    rest = lax.dot_general(a[1], b[:, :columns], dims, preferred_element_type=jnp.float32)
    return both[:, :columns] + both[:, columns:] + rest


def side_by_side(x):
    return jnp.concatenate(split(x), axis=1)


WHOLE = pl.BlockSpec(memory_space=pltpu.VMEM)
REMAIN = pl.BlockSpec(memory_space=pltpu.HBM)
CHEAP = pl.CostEstimate(flops=1, bytes_accessed=1, transcendentals=0)


def kernel_call(body, grid, in_specs, out_specs, out_shape, scratch=()):
    return pl.pallas_call(
        body,
        grid_spec=pltpu.PrefetchScalarGridSpec(
            num_scalar_prefetch=1, grid=grid, in_specs=in_specs, out_specs=out_specs, scratch_shapes=list(scratch)
        ),
        out_shape=out_shape,
        compiler_params=pltpu.CompilerParams(vmem_limit_bytes=VMEM),
        cost_estimate=CHEAP,
    )


def copies(table, blocks, buffers, sems):
    started = []
    for i, block in enumerate(blocks):
        pair = [pltpu.make_async_copy(table.at[(term, *block)], buffers.at[term, i], sems.at[term, i]) for term in range(2)]
        for copy in pair:
            copy.start()
        started.append(pair)
    return started


def fetched(refs, buffer, sems):
    started = [pltpu.make_async_copy(ref, buffer.at[i], sems.at[i]) for i, ref in enumerate(refs)]
    for copy in started:
        copy.start()
    return started


def arrived(pair):
    for copy in pair:
        copy.wait()


def transform(place, blocks, table):
    share, wide, wide2 = table.shape[1], *table.shape[-2:]
    channels = blocks[0].shape[-1]
    count = len(blocks)

    def body(place, *refs):
        ins, (table, out, x, v, sems, held, held_sems) = refs[:count], refs[count:]
        loads = fetched(ins, held, held_sems)
        pairs = copies(table, [(place[0], 0, i) for i in range(2 * share)], v, sems)
        for g in range(share):
            if count == 1:
                if g == 0:
                    arrived(loads)
                x[g] = side_by_side(held[0, g])
                continue
            arrived(loads[2 * g : 2 * g + 2])
            a, b = held[2 * g], held[2 * g + 1]
            swap = place[1] == 1
            size = 2 * a.shape[0]
            pair = jnp.concatenate([jnp.where(swap, b, a), jnp.where(swap, a, b)], axis=0)
            x[g, :size, :] = side_by_side(pair)
            x[g, size:, :] = jnp.zeros((wide2 - size, 2 * channels), BF16)
        for half in range(2):
            total = 0.0
            for g in range(share):
                i = half * share + g
                arrived(pairs[i])
                total += dot3((v[0, i], v[1, i]), x[g])
            out[half * wide : (half + 1) * wide, :] = total

    return kernel_call(
        body,
        (),
        [REMAIN] * (count + 1),
        WHOLE,
        jax.ShapeDtypeStruct((wide2, channels), jnp.float32),
        [
            pltpu.VMEM((share, wide2, 2 * channels), BF16),
            pltpu.VMEM((2, 2 * share, wide, wide2), BF16),
            pltpu.SemaphoreType.DMA((2, 2 * share)),
            pltpu.VMEM((count, *blocks[0].shape), jnp.float32),
            pltpu.SemaphoreType.DMA((count,)),
        ],
    )(place, *blocks, table)


def mix(place, rows, coef, weights, table, part_len, gradient=None):
    share, wide, wide2 = table.shape[1], *table.shape[-2:]
    deep, channels = weights.shape[0], weights.shape[1] // 2
    basis = deep // channels
    chunk = 16
    count = 2 * share
    rows = [*rows] + ([] if gradient is None else [gradient])
    n_rows = len(rows)
    n_in = n_rows + 3

    def body(place, *refs):
        coef, weights, table = refs[n_rows:n_in]
        ys, rest = refs[n_in : n_in + count], refs[n_in + count :]
        if gradient is not None:
            out, both, *rest = rest
        fh, fl, mixed, v, sems, held, held_sems, w, w_sems = rest
        loads = fetched(refs[:n_rows], held, held_sems)
        arrived(loads)
        w_loads = fetched((weights,), w, w_sems)
        blocks = [(place[0], 1, 2 * (i // 2) + (place[1] ^ (i % 2))) for i in range(count)]
        pairs = copies(table, blocks, v, sems)

        @pl.loop(0, wide // chunk, unroll=True)
        def _(i):
            re_at = pl.ds(pl.multiple_of(i * chunk, chunk), chunk)
            im_at = pl.ds(pl.multiple_of(wide + i * chunk, chunk), chunk)
            c = coef[re_at, :]
            data = [(held[d, re_at, :], held[d, im_at, :]) for d in range(3)]
            for k in range(basis):
                re, im = 0.0, 0.0
                for d, (xr, xi) in enumerate(data):
                    at = (d * basis + k) * 2
                    pr, pi = c[:, at : at + 1], c[:, at + 1 : at + 2]
                    re += pr * xr - pi * xi
                    im += pr * xi + pi * xr
                cols = pl.ds(k * channels, channels)
                fh[re_at, cols], fl[re_at, cols] = split(re)
                fh[im_at, cols], fl[im_at, cols] = split(im)

        arrived(w_loads)
        mixed[...] = side_by_side(dot3((fh[...], fl[...]), w[0]))
        for i, y in enumerate(ys):
            arrived(pairs[i])
            y[...] = dot3((v[0, i], v[1, i]), mixed[...])[:part_len]
        if gradient is not None:
            both[...] = side_by_side(held[3])
            for k in range(basis):
                at = pl.ds(k * channels, channels)
                out[at, :] = dot3((fh[:, at], fl[:, at]), both[...], (((0,), (0,)), ((), ())))

    y_shape = jax.ShapeDtypeStruct((part_len, channels), jnp.float32)
    extra, scratch = [], []
    if gradient is not None:
        extra = [jax.ShapeDtypeStruct((deep, channels), jnp.float32)]
        scratch = [pltpu.VMEM((wide2, 2 * channels), BF16)]
    return kernel_call(
        body,
        (),
        [REMAIN] * n_rows + [WHOLE] + [REMAIN] * 2,
        [WHOLE] * (count + len(extra)),
        [y_shape] * count + extra,
        scratch
        + [pltpu.VMEM((wide2, deep), BF16)] * 2
        + [pltpu.VMEM((wide2, 2 * channels), BF16)]
        + [pltpu.VMEM((2, count, wide, wide2), BF16), pltpu.SemaphoreType.DMA((2, count))]
        + [pltpu.VMEM((n_rows, wide2, channels), jnp.float32), pltpu.SemaphoreType.DMA((n_rows,))]
        + [pltpu.VMEM((1, deep, 2 * channels), BF16), pltpu.SemaphoreType.DMA((1,))],
    )(place, *rows, coef, weights, table)


def arrange(flags, got):
    part_len, channels = got[0].shape

    def body(flags, a, b, out):
        swap, full = flags[0] == 1, flags[1] == 1
        x, y = a[...], b[...]
        first, second = jnp.where(swap, y, x), jnp.where(swap, x, y)
        out[0] = jnp.where(full, first, first + second)
        out[1] = jnp.where(full, second, 0.0)

    return kernel_call(
        body,
        (),
        [WHOLE, WHOLE],
        WHOLE,
        jax.ShapeDtypeStruct((2, part_len, channels), jnp.float32),
    )(flags, *got)


def shares_sent(x, axis, me, ways, stride):
    parts = x.reshape(ways, -1, x.shape[-1])
    size = lax.axis_size(axis)
    pieces = [lax.dynamic_index_in_dim(parts, me, 0, keepdims=False)]
    for g in range(1, ways):
        piece = lax.dynamic_index_in_dim(parts, me ^ g, 0, keepdims=False)
        pieces.append(lax.ppermute(piece, axis, [(a, a ^ (g * stride)) for a in range(size)]))
    return pieces


def shares_summed(pieces):
    total = pieces[0]
    for piece in pieces[1:]:
        total = total + piece
    return total


def share_shown(x, axis, ways, stride):
    size = lax.axis_size(axis)
    return [x] + [lax.ppermute(x, axis, [(a, a ^ (g * stride)) for a in range(size)]) for g in range(1, ways)]


def shares_joined(pieces, me):
    ways = len(pieces)
    whole = jnp.zeros((ways,) + pieces[0].shape, pieces[0].dtype)
    for g, piece in enumerate(pieces):
        whole = lax.dynamic_update_index_in_dim(whole, piece, me ^ g, 0)
    return whole.reshape((-1,) + pieces[0].shape[1:])


def make_local(lat, lon):
    lay = Layout(lat, lon)
    share = lay.share

    def send(x, pairs):
        return lax.ppermute(x, AXES, pairs)

    def local(signal, band_rows, filter_modes, mixing, cotangent):
        channels = signal.shape[2]
        part_len = signal.shape[1]
        length = part_len * lon
        modes = filter_modes.shape[-1]
        basis = mixing.shape[0]
        width = modes // share

        band = lax.axis_index("lat")
        z = lax.axis_index("lon")
        core = band % 2
        v = jnp.where((band // 2) % 2 == 0, z, lon - 1 - z)
        rho = v // lay.chips
        h = (v % lay.chips) * 2 + core
        r_held = rho % 2
        live = lax.dynamic_index_in_dim(band_rows, band, 0, keepdims=False)
        full = live == 2
        high_z = z // share

        table, wide = tables(length, modes, lon, share)
        table = jnp.asarray(table)
        place = jnp.stack([h, r_held]).astype(jnp.int32)
        flags = jnp.stack([high_z, full.astype(jnp.int32)]).astype(jnp.int32)

        def fetch(x, then=None):
            got = []
            for t in range(2):
                row = jnp.minimum(high_z ^ t, live - 1)
                message = lax.dynamic_index_in_dim(x, row, 0, keepdims=False)
                if then is not None:
                    message = after(message, *then)
                got.append(send(message, lay.inward(t)))
            return got

        def enter(got):
            blocks = list(got)
            for g in range(1, share):
                blocks += [send(x, lay.within(g)) for x in got]
            if part_len % 8:
                pairs = []
                for x, y in zip(blocks[::2], blocks[1::2]):
                    pairs += [jnp.where(r_held == 0, x, y), jnp.where(r_held == 0, y, x)]
                blocks = jnp.concatenate(pairs, axis=0).reshape(share, 2 * part_len, channels)
                blocks = [jnp.pad(blocks, ((0, 0), (0, 2 * (wide - part_len)), (0, 0)))]
            return transform(place, blocks, table)

        def exchange(y):
            return [[send(y[2 * g + t], lay.within(g)) for t in range(2)] for g in range(1, share)]

        def total(own, others):
            return [own[t] + sum(other[t] for other in others) for t in range(2)]

        def deliver(block, t):
            return send(block, flipped(lay.inward(t)))

        def halo(spec):
            return send(spec, lay.upward()), send(spec, flipped(lay.upward()))

        s_got = fetch(signal)
        f = after(filter_modes, *s_got)
        ladder = [(i, i + 1) for i in range(lat - 1)]
        below = lax.ppermute(jnp.where(full, f[1, 2], f[0, 2]), "lat", ladder)
        above = lax.ppermute(f[0, 0], "lat", flipped(ladder))
        nil = jnp.zeros_like(below)
        is_first = r_held == 0
        ahead = [
            jnp.where(is_first, f[0, 0], jnp.where(full, f[1, 0], nil)),
            jnp.where(is_first, f[0, 1], jnp.where(full, f[1, 1], nil)),
            jnp.where(is_first, jnp.where(full, f[0, 2], nil), jnp.where(full, f[1, 2], f[0, 2])),
        ]
        back = [
            jnp.where(is_first, below, jnp.where(full, f[0, 2], nil)),
            jnp.where(is_first, f[0, 1], jnp.where(full, f[1, 1], nil)),
            jnp.where(is_first, jnp.where(full, f[1, 0], nil), above),
        ]
        conj = jnp.array([1.0, -1.0], jnp.float32)[None, None, :, None]
        both = jnp.stack([jnp.stack(ahead), jnp.stack(back) * conj])
        both = both.reshape(2 * 3 * basis * 2, modes)
        swap = [(i, i ^ 1) for i in range(lat)]
        theirs = lax.ppermute(lax.dynamic_slice_in_dim(both, (h ^ 1) * width, width, 1), "lat", swap)
        mine = lax.dynamic_slice_in_dim(both, h * width, width, 1)
        coef = jnp.where(rho // 2 == core, mine, theirs).reshape(2, 3 * basis * 2, width)
        coef = jnp.pad(jnp.transpose(coef, (0, 2, 1)), ((0, 0), (0, wide - width), (0, 0)))

        flat = (basis * channels, channels)
        ahead_weights = split_outside(mixing.reshape(flat))
        back_weights = split_outside(jnp.transpose(mixing, (0, 2, 1)).reshape(flat))

        pair = band // 2
        even = (basis * channels // lat) * channels % (lon * 128) == 0

        def swap_core(x):
            return lax.ppermute(x, "lat", swap)

        s_got = [after(x, ahead_weights, back_weights) for x in s_got]
        g_got = fetch(cotangent, s_got)
        s_spec = enter(s_got)
        g_got = [after(x, s_spec, coef) for x in g_got]
        s_halo = halo(s_spec)
        g_spec = enter(g_got)
        s_halo = [after(x, g_spec) for x in s_halo]
        g_halo = halo(g_spec)
        *y, term = mix(place, (s_halo[0], s_spec, s_halo[1]), coef[0], ahead_weights, table, part_len, g_spec)
        g_halo = [after(x, *y) for x in g_halo]
        others = exchange(y)
        halves = term.reshape(2, -1, channels)
        give = after(lax.dynamic_index_in_dim(halves, 1 - core, 0, keepdims=False), *g_halo, *[x for other in others for x in other])
        given = swap_core(give)
        o_blocks = total(y, others)

        o_got = [deliver(x, t) for t, x in enumerate(o_blocks)]
        term = lax.dynamic_index_in_dim(halves, core, 0, keepdims=False) + after(given, *o_blocks)
        pieces = shares_sent(term, "lat", pair, lay.pairs, 2)
        g_halo = [after(x, *o_blocks, term) for x in g_halo]
        y = mix(place, (g_halo[0], g_spec, g_halo[1]), coef[1], back_weights, table, part_len)
        o_got = [after(x, *y) for x in o_got]
        y = [after(x, o_got[0]) for x in y]
        others = [[after(x, *o_got) for x in other] for other in exchange(y)]
        term = shares_summed([after(x, *y) for x in pieces])
        term_shape = term.shape
        term = term.reshape((-1, 128) if even else (lon, -1))
        pieces = shares_sent(term, "lon", z, lon, 1)
        b_blocks = total(y, others)
        term = shares_summed([after(x, *b_blocks) for x in pieces])
        b_got = [deliver(after(x, term), t) for t, x in enumerate(b_blocks)]
        term = shares_joined(share_shown(term, "lon", lon, 1), z).reshape(term_shape)
        output = arrange(flags, o_got)
        b_got = [after(x, output) for x in b_got]
        term = shares_joined([after(x, b_got[0]) for x in share_shown(term, "lat", lay.pairs, 2)], pair)
        b_got[1] = after(b_got[1], term)
        other = swap_core(after(term, b_got[1]))
        grad_signal = arrange(flags, b_got)
        term = jnp.concatenate([jnp.where(core == 0, term, other), jnp.where(core == 0, other, term)], axis=0)
        weight_grad = term.reshape(mixing.shape)
        return output, grad_signal, weight_grad

    return local


def solution(mesh):
    lat, lon = mesh.shape["lat"], mesh.shape["lon"]
    grid = P("lat", "lon", None)
    return jax.shard_map(
        make_local(lat, lon),
        mesh=mesh,
        in_specs=(grid, P(), P("lat", None, None, None, None), P(), grid),
        out_specs=(grid, grid, P()),
        check_vma=False,
    )
```
